32 devices in a mesh: dp: 8 (over z, core), seq: 4 (over y, x).
Axes of the slice: x: 2, y: 2, z: 4, core: 2. Of those that a mesh axis runs over, the one named last changes fastest.
Arguments:
- tokens: bfloat16 [8192, 2304], P(('dp', 'seq')), may hold values from -6 to 6
- query_weight: bfloat16 [2304, 2048], P('dp', 'seq'), may hold values from -0.125 to 0.125
- key_weight: bfloat16 [2304, 1024], P('dp', 'seq'), may hold values from -0.125 to 0.125
- value_weight: bfloat16 [2304, 1024], P('dp', 'seq'), may hold values from -0.125 to 0.125
- output_weight: bfloat16 [2304, 2048], P('dp', 'seq'), may hold values from -0.125 to 0.125
- attn_norm: bfloat16 [2304], P('dp'), may hold values from -0.5 to 0.5
- post_attn_norm: bfloat16 [2304], P('dp'), may hold values from -0.5 to 0.5
- ffn_norm: bfloat16 [2304], P('dp'), may hold values from -0.5 to 0.5
- post_ffn_norm: bfloat16 [2304], P('dp'), may hold values from -0.5 to 0.5
- gate_weight: bfloat16 [2304, 9216], P('dp', 'seq'), may hold values from -0.125 to 0.125
- up_weight: bfloat16 [2304, 9216], P('dp', 'seq'), may hold values from -0.125 to 0.125
- down_weight: bfloat16 [2304, 9216], P('dp', 'seq'), may hold values from -0.0625 to 0.0625
- cotangent: bfloat16 [8192, 2304], P(('dp', 'seq')), may hold values from -6 to 6
Outputs:
- result: bfloat16 [8192, 2304], P(('dp', 'seq'))
- grad_tokens: float32 [8192, 2304], P(('dp', 'seq'))
- grad_query: float32 [2304, 2048], P('dp', 'seq')
- grad_key: float32 [2304, 1024], P('dp', 'seq')
- grad_value: float32 [2304, 1024], P('dp', 'seq')
- grad_output: float32 [2304, 2048], P('dp', 'seq')
- grad_attn_norm: float32 [2304], P(('dp', 'seq'))
- grad_post_attn_norm: float32 [2304], P(('dp', 'seq'))
- grad_ffn_norm: float32 [2304], P(('dp', 'seq'))
- grad_post_ffn_norm: float32 [2304], P(('dp', 'seq'))
- grad_gate: float32 [2304, 9216], P('dp', 'seq')
- grad_up: float32 [2304, 9216], P('dp', 'seq')
- grad_down: float32 [2304, 9216], P('dp', 'seq')
The draws below stay inside these ranges and needn't reach their ends.
All inputs are finite; a program needn't handle non-finite values.
Results may differ from the reference program's by a relative error of at most 0.023.
Values may be sent and summed in bfloat16 or wider, within the bound.
No kernel may reach another device: no remote copies, remote signals or barrier semaphores. Data moves between devices by JAX's collectives and lax.ppermute only.
A program may use at most 320 MiB of HBM per device.

```python
import jax
import jax.numpy as jnp
from jax import lax

D = 2304
HQ = 8
HK = 4
HD = 256
FF = 9216
WINDOW = 4096
SEQ_LEN = 1024
TOKENS = 8192
N_DP = 8


def block_scale(key, shape, pieces, low, top_value):
    loudness = 1.0
    for axis_at, blocks in pieces:
        draws = jax.random.uniform(jax.random.fold_in(jax.random.fold_in(key, 6), axis_at), (blocks,), jnp.float32, low / len(pieces), top_value / len(pieces))
        loudness = loudness * jnp.repeat(jnp.exp(draws), shape[axis_at] // blocks).reshape((-1,) + (1,) * (len(shape) - 1 - axis_at))
    return loudness


def noise(stream_key, shape, spread, most, pieces=(), dtype=jnp.bfloat16):
    entries = spread * jax.random.normal(stream_key, shape, jnp.float32)
    if pieces:
        entries = entries * block_scale(stream_key, shape, pieces, -0.22, 0.18)
    return jnp.clip(entries, -most, most).astype(dtype)


def setup_inputs(seed: int = 0) -> dict:
    arg_keys = jax.random.split(jax.random.key(seed), 14)
    return {
        "tokens": noise(arg_keys[0], (TOKENS, D), 1.0, 6.0, ((0, 32),)),
        "query_weight": noise(arg_keys[1], (D, HQ * HD), D ** -0.5, 0.125, ((0, 8), (1, 4))),
        "key_weight": noise(arg_keys[2], (D, HK * HD), D ** -0.5, 0.125, ((0, 8), (1, 4))),
        "value_weight": noise(arg_keys[3], (D, HK * HD), D ** -0.5, 0.125, ((0, 8), (1, 4))),
        "output_weight": noise(arg_keys[4], (D, HQ * HD), (HQ * HD) ** -0.5, 0.125, ((0, 8), (1, 4))),
        "attn_norm": jnp.clip(jax.random.uniform(arg_keys[5], (D,), jnp.float32, -0.5, 0.5) * block_scale(arg_keys[5], (D,), ((0, 8),), -0.4, 0.0), -0.5, 0.5).astype(jnp.bfloat16),
        "post_attn_norm": jnp.clip(jax.random.uniform(arg_keys[6], (D,), jnp.float32, -0.5, 0.5) * block_scale(arg_keys[6], (D,), ((0, 8),), -0.4, 0.0), -0.5, 0.5).astype(jnp.bfloat16),
        "ffn_norm": jnp.clip(jax.random.uniform(arg_keys[7], (D,), jnp.float32, -0.5, 0.5) * block_scale(arg_keys[7], (D,), ((0, 8),), -0.4, 0.0), -0.5, 0.5).astype(jnp.bfloat16),
        "post_ffn_norm": jnp.clip(jax.random.uniform(arg_keys[8], (D,), jnp.float32, -0.5, 0.5) * block_scale(arg_keys[8], (D,), ((0, 8),), -0.4, 0.0), -0.5, 0.5).astype(jnp.bfloat16),
        "gate_weight": noise(arg_keys[9], (D, FF), D ** -0.5, 0.125, ((0, 8), (1, 4))),
        "up_weight": noise(arg_keys[10], (D, FF), D ** -0.5, 0.125, ((0, 8), (1, 4))),
        "down_weight": noise(arg_keys[11], (D, FF), FF ** -0.5, 0.0625, ((0, 8), (1, 4))),
        "cotangent": noise(arg_keys[12], (TOKENS, D), 1.0, 6.0, ((0, 32),)),
    }


@jax.custom_vjp
def low(v):
    return lax.optimization_barrier(v.astype(jnp.bfloat16)).astype(jnp.float32)

@jax.custom_vjp
def low_back(v):
    return v

def low_keep(v):
    return (low(v), None)

def low_pass(kept, grad):
    return (grad,)

def back_keep(v):
    return (v, None)

def back_low(kept, grad):
    return (low(grad),)
low.defvjp(low_keep, low_pass)
low_back.defvjp(back_keep, back_low)
HIGH = lax.Precision.HIGHEST
EPSILON = 1e-06
SOFT_CAP = 50.0

def norm_rows(values, scales):
    factor = lax.rsqrt(lax.optimization_barrier(jnp.mean(values * values, axis=-1, keepdims=True)) + EPSILON)
    return values * factor * (1.0 + scales)

def rotate(values, offset):
    count = values.shape[0]
    half = values.shape[2] // 2
    places = (offset + jnp.arange(count)).astype(jnp.float32)
    freqs = 10000.0 ** (-jnp.arange(half).astype(jnp.float32) / half)
    angles = places[:, None] * freqs[None, :]
    cosine = jnp.cos(angles)[:, None, :]
    sine = jnp.sin(angles)[:, None, :]
    left = values[..., :half]
    right = values[..., half:]
    return jnp.concatenate([left * cosine - right * sine, right * cosine + left * sine], axis=-1)

def attend(queries, keys, values):
    length, heads, size = queries.shape
    block = min(512, length)
    count = length // block
    columns = jnp.arange(length)

    def single(item):
        start, q_part = item
        raw = jnp.einsum('qhd,khd->hqk', q_part, keys, precision=HIGH)
        scores = low_back(raw)
        capped = SOFT_CAP * jnp.tanh(scores / SOFT_CAP)
        rows_now = start + jnp.arange(block)
        allowed = (columns[None, :] <= rows_now[:, None]) & (rows_now[:, None] - columns[None, :] < WINDOW)
        masked = jnp.where(allowed[None], capped, -1e+30)
        highest = lax.optimization_barrier(jnp.max(masked, axis=-1, keepdims=True))
        weights = jnp.exp(masked - highest)
        probs = weights / lax.optimization_barrier(jnp.sum(weights, axis=-1, keepdims=True))
        return jnp.einsum('hqk,khd->qhd', low(probs), values, precision=HIGH)
    starts = jnp.arange(count) * block
    outputs = lax.map(jax.checkpoint(single), (starts, queries.reshape(count, block, heads, size)))
    return outputs.reshape(length, heads, size)

def decoder_layer(inputs, w_query, w_key, w_value, w_output, scale_one, scale_two, scale_three, scale_four, w_gate, w_up, w_down):
    length = inputs.shape[0]
    groups = HQ // HK
    normed = low(norm_rows(inputs, scale_one))
    q_lin = jnp.dot(normed, w_query, precision=HIGH).reshape(length, HQ, HD)
    k_lin = jnp.dot(normed, w_key, precision=HIGH).reshape(length, HK, HD)
    v_lin = jnp.dot(normed, w_value, precision=HIGH).reshape(length, HK, HD)
    queries = low(rotate(low_back(q_lin), 0) * HD ** (-0.5))
    keys = low(rotate(low_back(jnp.repeat(k_lin, groups, axis=1)), 0))
    values = low(low_back(jnp.repeat(v_lin, groups, axis=1)))
    mixed = low_back(low(attend(queries, keys, values))).reshape(length, HQ * HD)
    projected = low_back(jnp.dot(mixed, w_output.T, precision=HIGH))
    hidden = inputs + norm_rows(projected, scale_two)
    ffn_in = low(norm_rows(hidden, scale_three))
    gate = low_back(jnp.dot(ffn_in, w_gate, precision=HIGH))
    upward = low_back(jnp.dot(ffn_in, w_up, precision=HIGH))
    inner = low(jax.nn.gelu(gate, approximate=True) * upward)
    ffn_raw = low_back(jnp.dot(inner, w_down.T, precision=HIGH))
    return hidden + norm_rows(ffn_raw, scale_four)

def reference(tokens, query_weight, key_weight, value_weight, output_weight, attn_norm, post_attn_norm, ffn_norm, post_ffn_norm, gate_weight, up_weight, down_weight, cotangent):
    floats = tuple((item.astype(jnp.float32) for item in (tokens, query_weight, key_weight, value_weight, output_weight, attn_norm, post_attn_norm, ffn_norm, post_ffn_norm, gate_weight, up_weight, down_weight)))

    def forward(inputs, *weights):
        sequences = inputs.reshape(N_DP, SEQ_LEN, D)
        checked = jax.checkpoint(decoder_layer)

        def advance(carry, sequence):
            return (carry, checked(sequence, *weights))
        unused, outputs = lax.scan(advance, jnp.zeros((), jnp.float32), sequences)
        return outputs.reshape(TOKENS, D)
    outcome, pull_back = jax.vjp(forward, *floats)
    grads = pull_back(cotangent.astype(jnp.float32))
    return (outcome.astype(jnp.bfloat16), grads[0], grads[1], grads[2], grads[3], grads[4], grads[5], grads[6], grads[7], grads[8], grads[9], grads[10], grads[11])
```

```python
import jax
import jax.numpy as jnp
from jax import lax
from jax.sharding import PartitionSpec as P

HQ = 8
HK = 4
HD = 256
WINDOW = 4096
EPSILON = 1e-06
SOFT_CAP = 50.0
LOW = jnp.bfloat16
WIDE = jnp.float32


def swap_pairs(count, mask):
    return [(i, i ^ mask) for i in range(count)]


def gather_small(values, axis):
    count = lax.axis_size(axis)
    if count & (count - 1):
        return lax.all_gather(values, axis, axis=0, tiled=False)
    place = lax.axis_index(axis)
    held = values[None]
    bit = 1
    while bit < count:
        other = lax.ppermute(held, axis, swap_pairs(count, bit))
        upper = (place & bit) != 0
        held = jnp.where(
            upper, jnp.concatenate([other, held]), jnp.concatenate([held, other])
        )
        bit *= 2
    return held


def scatter_small(values, axis):
    count = lax.axis_size(axis)
    if count & (count - 1):
        return lax.psum_scatter(values, axis, scatter_dimension=0, tiled=False)
    place = lax.axis_index(axis)
    bit = count // 2
    while bit:
        halves = values.reshape((2, bit) + values.shape[1:])
        upper = (place & bit) != 0
        keep = jnp.where(upper, halves[1], halves[0])
        send = jnp.where(upper, halves[0], halves[1])
        values = keep + lax.ppermute(send, axis, swap_pairs(count, bit))
        bit //= 2
    return values[0]


def square(count):
    return count == 4


def chunk_places(count):
    here = lax.axis_index("seq")
    if square(count):
        return here ^ jnp.arange(count)
    return jnp.arange(count)


def gather_rows(rows):
    count = lax.axis_size("seq")
    if not square(count):
        return lax.all_gather(rows, "seq", axis=0, tiled=True)
    half = rows.shape[0] // 2
    along, across = swap_pairs(count, 1), swap_pairs(count, 2)
    from_x = lax.ppermute(rows, "seq", along)
    from_y = lax.ppermute(rows, "seq", across)
    far_top = lax.ppermute(from_y[:half], "seq", along)
    far_low = lax.ppermute(from_x[half:], "seq", across)
    return jnp.concatenate([rows, from_x, from_y, far_top, far_low])


def scatter_rows(partial, size):
    count = lax.axis_size("seq")
    if not square(count):
        return lax.psum_scatter(
            partial(0, count * size).astype(LOW), "seq", scatter_dimension=0, tiled=True
        ).astype(WIDE)
    half = size // 2
    along, across = swap_pairs(count, 1), swap_pairs(count, 2)
    far = partial(3 * size, 4 * size).astype(LOW)
    via_x = lax.ppermute(far[:half], "seq", along)
    via_y = lax.ppermute(far[half:], "seq", across)
    to_x = partial(size, 2 * size)
    to_y = partial(2 * size, 3 * size)
    to_x = jnp.concatenate([to_x[:half], to_x[half:] + via_y.astype(WIDE)]).astype(LOW)
    to_y = jnp.concatenate([to_y[:half] + via_x.astype(WIDE), to_y[half:]]).astype(LOW)
    from_x = lax.ppermute(to_x, "seq", along)
    from_y = lax.ppermute(to_y, "seq", across)
    own = partial(0, size)
    return own + from_x.astype(WIDE) + from_y.astype(WIDE)


def gather_width(shard):
    return lax.all_gather(shard, "dp", axis=0, tiled=True)


def scatter_width(grad):
    return lax.psum_scatter(grad.astype(LOW), "dp", scatter_dimension=0, tiled=True).astype(WIDE)


def dot(left, right):
    return jnp.dot(left, right, preferred_element_type=WIDE)


def dot_last(left, right):
    return lax.dot_general(left, right, (((1,), (1,)), ((), ())), preferred_element_type=WIDE)


def dot_first(left, right):
    return lax.dot_general(left, right, (((0,), (0,)), ((), ())), preferred_element_type=WIDE)


def norm_factor(values):
    return lax.rsqrt(jnp.mean(values * values, axis=-1, keepdims=True) + EPSILON)


def norm_back(values, factor, scale, grad):
    scaled = grad * scale
    inner = jnp.mean(scaled * values, axis=-1, keepdims=True)
    back = factor * scaled - values * (factor * factor * factor * inner)
    return back, jnp.sum(grad * values * factor, axis=0)


def rotate(values, cosine, sine):
    half = values.shape[1] // 2
    left = values[:, :half]
    right = values[:, half:]
    return jnp.concatenate([left * cosine - right * sine, right * cosine + left * sine], axis=1)


def gelu_parts(gate):
    scale = 0.7978845608028654
    square_gate = gate * gate
    turn = jnp.tanh(scale * (gate + 0.044715 * (square_gate * gate)))
    value = 0.5 * gate * (1.0 + turn)
    slope = 0.5 * (1.0 + turn) + 0.5 * gate * (1.0 - turn * turn) * (
        scale * (1.0 + 3.0 * 0.044715 * square_gate)
    )
    return value, slope


def shards(
    tokens,
    query_weight,
    key_weight,
    value_weight,
    output_weight,
    attn_norm,
    post_attn_norm,
    ffn_norm,
    post_ffn_norm,
    gate_weight,
    up_weight,
    down_weight,
    cotangent,
):
    size, width = tokens.shape
    seq_count = lax.axis_size("seq")
    dp_count = lax.axis_size("dp")
    heads = HQ // seq_count
    sharing = max(1, seq_count // HK)
    groups = [[first + i for i in range(sharing)] for first in range(0, seq_count, sharing)]
    kv_heads = max(1, HK // seq_count)
    copies = heads // kv_heads

    if sharing > 1:
        key_weight = lax.all_gather(
            key_weight, "seq", axis=1, tiled=True, axis_index_groups=groups
        )
        value_weight = lax.all_gather(
            value_weight, "seq", axis=1, tiled=True, axis_index_groups=groups
        )
    q_cols, kv_cols = heads * HD, kv_heads * HD
    mine = jnp.concatenate([query_weight, key_weight, value_weight], axis=1)
    w_qkv = gather_width(mine)
    w_output = gather_width(output_weight)
    w_gate = gather_width(gate_weight)
    w_up = gather_width(up_weight)
    w_down = gather_width(down_weight)

    stacked = jnp.stack([attn_norm, post_attn_norm, ffn_norm, post_ffn_norm])
    scales = gather_small(stacked, "dp").transpose(1, 0, 2).reshape(4, width)
    scales = 1.0 + scales.astype(WIDE)
    scale_one, scale_two, scale_three, scale_four = (scales[i : i + 1] for i in range(4))

    whole_tokens = gather_rows(tokens).astype(WIDE)
    normed = (whole_tokens * norm_factor(whole_tokens) * scale_one).astype(LOW)
    length = size * seq_count
    places = (chunk_places(seq_count)[:, None] * size + jnp.arange(size)[None, :]).reshape(length)
    half = HD // 2
    freqs = 10000.0 ** (-jnp.arange(half).astype(WIDE) / half)
    angles = places.astype(WIDE)[:, None] * freqs[None, :]
    cosine, sine = jnp.cos(angles), jnp.sin(angles)
    allowed = (places[None, :] <= places[:, None]) & (
        places[:, None] - places[None, :] < WINDOW
    )
    q_scale = HD ** (-0.5)
    linear = dot(normed, w_qkv)
    queries = [
        (rotate(linear[:, h * HD : (h + 1) * HD], cosine, sine) * q_scale).astype(LOW)
        for h in range(heads)
    ]
    keys = [
        rotate(linear[:, q_cols + j * HD : q_cols + (j + 1) * HD], cosine, sine).astype(LOW)
        for j in range(kv_heads)
    ]
    first_value = q_cols + kv_cols
    values = [
        linear[:, first_value + j * HD : first_value + (j + 1) * HD].astype(LOW)
        for j in range(kv_heads)
    ]
    probs, turns, head_outs = [], [], []
    for h in range(heads):
        turn = jnp.tanh(dot_last(queries[h], keys[h // copies]) / SOFT_CAP)
        capped = jnp.where(allowed, SOFT_CAP * turn, -1e30)
        highest = jnp.max(capped, axis=-1, keepdims=True)
        weights = jnp.exp(capped - highest)
        prob = weights / jnp.sum(weights, axis=-1, keepdims=True)
        probs.append(prob)
        turns.append(turn)
        head_outs.append(dot(prob.astype(LOW), values[h // copies]).astype(LOW))
    mixed = jnp.concatenate(head_outs, axis=1)
    projected = scatter_rows(lambda a, b: dot_last(mixed[a:b], w_output), size)

    inputs = tokens.astype(WIDE)
    factor_two = norm_factor(projected)
    hidden = inputs + projected * factor_two * scale_two
    factor_three = norm_factor(hidden)
    whole_in = gather_rows((hidden * factor_three * scale_three).astype(LOW))
    gate = dot(whole_in, w_gate)
    upward = dot(whole_in, w_up)
    activated, slope = gelu_parts(gate)
    inner = (activated * upward).astype(LOW)
    ffn_raw = scatter_rows(lambda a, b: dot_last(inner[a:b], w_down), size)
    factor_four = norm_factor(ffn_raw)
    result = (hidden + ffn_raw * factor_four * scale_four).astype(LOW)

    grad_result = cotangent.astype(WIDE)
    grad_raw, grad_scale_four = norm_back(ffn_raw, factor_four, scale_four, grad_result)
    whole_grad = gather_rows(grad_raw.astype(LOW))
    shard_down = scatter_width(dot_first(whole_grad, inner))
    grad_inner = dot(whole_grad, w_down)
    grad_gate = (grad_inner * upward * slope).astype(LOW)
    grad_up = (grad_inner * activated).astype(LOW)
    shard_gate = scatter_width(dot_first(whole_in, grad_gate))
    shard_up = scatter_width(dot_first(whole_in, grad_up))
    grad_ffn_in = scatter_rows(
        lambda a, b: dot_last(grad_gate[a:b], w_gate) + dot_last(grad_up[a:b], w_up), size
    )
    back_three, grad_scale_three = norm_back(hidden, factor_three, scale_three, grad_ffn_in)
    grad_hidden = grad_result + back_three
    back_two, grad_scale_two = norm_back(projected, factor_two, scale_two, grad_hidden)
    whole_proj = gather_rows(back_two.astype(LOW))
    shard_output = scatter_width(dot_first(whole_proj, mixed))
    grad_mixed = dot(whole_proj, w_output).astype(LOW)

    grad_q, grad_k, grad_v = [], [0.0] * kv_heads, [0.0] * kv_heads
    for h in range(heads):
        j = h // copies
        grad_head = grad_mixed[:, h * HD : (h + 1) * HD]
        grad_probs = dot_last(grad_head, values[j])
        across = jnp.sum(grad_probs * probs[h], axis=-1, keepdims=True)
        grad_scores = (
            probs[h] * (grad_probs - across) * (1.0 - turns[h] * turns[h])
        ).astype(LOW)
        grad_q.append(
            (rotate(dot(grad_scores, keys[j]), cosine, -sine) * q_scale).astype(LOW)
        )
        grad_k[j] = grad_k[j] + dot_first(grad_scores, queries[h])
        grad_v[j] = grad_v[j] + dot_first(probs[h].astype(LOW), grad_head)
    grad_k = [rotate(item, cosine, -sine).astype(LOW) for item in grad_k]
    grad_v = [item.astype(LOW) for item in grad_v]
    grad_linear = jnp.concatenate(grad_q + grad_k + grad_v, axis=1)
    shard_qkv = scatter_width(dot_first(normed, grad_linear))
    grad_normed = scatter_rows(lambda a, b: dot_last(grad_linear[a:b], w_qkv), size)
    back_one, grad_scale_one = norm_back(inputs, norm_factor(inputs), scale_one, grad_normed)
    grad_tokens = grad_hidden + back_one

    shard_query = shard_qkv[:, :q_cols]
    shard_key = shard_qkv[:, q_cols:first_value]
    shard_value = shard_qkv[:, first_value:]
    if sharing > 1:
        shard_key, shard_value = (
            lax.psum_scatter(
                item.astype(LOW),
                "seq",
                scatter_dimension=1,
                tiled=True,
                axis_index_groups=groups,
            ).astype(WIDE)
            for item in (shard_key, shard_value)
        )

    piece = width // (dp_count * seq_count)
    stacked = jnp.stack([grad_scale_one, grad_scale_two, grad_scale_three, grad_scale_four])
    packed = stacked.reshape(4, dp_count, seq_count, piece).transpose(1, 2, 0, 3)
    packed = packed.reshape(dp_count, seq_count, 4 * piece)
    owned = scatter_small(scatter_small(packed, "dp"), "seq").reshape(4, piece)
    return (
        result,
        grad_tokens,
        shard_query,
        shard_key,
        shard_value,
        shard_output,
        owned[0],
        owned[1],
        owned[2],
        owned[3],
        shard_gate,
        shard_up,
        shard_down,
    )


def solution(mesh):
    rows = P(("dp", "seq"), None)
    weight = P("dp", "seq")
    scale = P("dp")
    scale_grad = P(("dp", "seq"))
    in_specs = (
        (rows,) + (weight,) * 4 + (scale,) * 4 + (weight,) * 3 + (rows,)
    )
    out_specs = (rows, rows) + (weight,) * 4 + (scale_grad,) * 4 + (weight,) * 3
    return jax.shard_map(
        shards, mesh=mesh, in_specs=in_specs, out_specs=out_specs, check_vma=False
    )
```

```python
import jax
import jax.numpy as jnp
from jax import lax
from jax.sharding import PartitionSpec as P

HQ = 8
HK = 4
HD = 256
WINDOW = 4096
EPSILON = 1e-06
SOFT_CAP = 50.0
LOW = jnp.bfloat16
WIDE = jnp.float32


def swap_pairs(count, mask):
    return [(i, i ^ mask) for i in range(count)]


def gather_small(values, axis):
    count = lax.axis_size(axis)
    if count & (count - 1):
        return lax.all_gather(values, axis, axis=0, tiled=False)
    place = lax.axis_index(axis)
    held = values[None]
    bit = 1
    while bit < count:
        other = lax.ppermute(held, axis, swap_pairs(count, bit))
        upper = (place & bit) != 0
        held = jnp.where(
            upper, jnp.concatenate([other, held]), jnp.concatenate([held, other])
        )
        bit *= 2
    return held


def scatter_small(values, axis):
    count = lax.axis_size(axis)
    if count & (count - 1):
        return lax.psum_scatter(values, axis, scatter_dimension=0, tiled=False)
    place = lax.axis_index(axis)
    bit = count // 2
    while bit:
        halves = values.reshape((2, bit) + values.shape[1:])
        upper = (place & bit) != 0
        keep = jnp.where(upper, halves[1], halves[0])
        send = jnp.where(upper, halves[0], halves[1])
        values = keep + lax.ppermute(send, axis, swap_pairs(count, bit))
        bit //= 2
    return values[0]


def square(count):
    return count == 4


def chunk_places(count):
    here = lax.axis_index("seq")
    if square(count):
        return here ^ jnp.arange(count)
    return jnp.arange(count)


def gather_rows(rows):
    count = lax.axis_size("seq")
    if not square(count):
        return lax.all_gather(rows, "seq", axis=0, tiled=True)
    half = rows.shape[0] // 2
    along, across = swap_pairs(count, 1), swap_pairs(count, 2)
    from_x = lax.ppermute(rows, "seq", along)
    from_y = lax.ppermute(rows, "seq", across)
    far_top = lax.ppermute(from_y[:half], "seq", along)
    far_low = lax.ppermute(from_x[half:], "seq", across)
    return jnp.concatenate([rows, from_x, from_y, far_top, far_low])


def scatter_rows(partial, size):
    count = lax.axis_size("seq")
    if not square(count):
        return lax.psum_scatter(
            partial(0, count * size).astype(LOW), "seq", scatter_dimension=0, tiled=True
        ).astype(WIDE)
    half = size // 2
    along, across = swap_pairs(count, 1), swap_pairs(count, 2)
    far = partial(3 * size, 4 * size).astype(LOW)
    via_x = lax.ppermute(far[:half], "seq", along)
    via_y = lax.ppermute(far[half:], "seq", across)
    to_x = partial(size, 2 * size)
    to_y = partial(2 * size, 3 * size)
    to_x = jnp.concatenate([to_x[:half], to_x[half:] + via_y.astype(WIDE)]).astype(LOW)
    to_y = jnp.concatenate([to_y[:half] + via_x.astype(WIDE), to_y[half:]]).astype(LOW)
    from_x = lax.ppermute(to_x, "seq", along)
    from_y = lax.ppermute(to_y, "seq", across)
    own = partial(0, size)
    return own + from_x.astype(WIDE) + from_y.astype(WIDE)


def gather_width(shard):
    return lax.all_gather(shard, "dp", axis=0, tiled=True)


def hold_first(grad, later):
    return lax.optimization_barrier((grad.astype(LOW), later))


def scatter_width(grad, before=None):
    if before is not None:
        grad, before = lax.optimization_barrier((grad, before))
    total = lax.psum_scatter(grad, "dp", scatter_dimension=0, tiled=True)
    return total, before


def dot(left, right):
    return jnp.dot(left, right, preferred_element_type=WIDE)


def dot_last(left, right):
    return lax.dot_general(left, right, (((1,), (1,)), ((), ())), preferred_element_type=WIDE)


def dot_first(left, right):
    return lax.dot_general(left, right, (((0,), (0,)), ((), ())), preferred_element_type=WIDE)


def norm_factor(values):
    return lax.rsqrt(jnp.mean(values * values, axis=-1, keepdims=True) + EPSILON)


def norm_back(values, factor, scale, grad):
    scaled = grad * scale
    inner = jnp.mean(scaled * values, axis=-1, keepdims=True)
    back = factor * scaled - values * (factor * factor * factor * inner)
    return back, jnp.sum(grad * values * factor, axis=0)


def rotate(values, cosine, sine):
    half = values.shape[1] // 2
    left = values[:, :half]
    right = values[:, half:]
    return jnp.concatenate([left * cosine - right * sine, right * cosine + left * sine], axis=1)


def gelu_parts(gate):
    scale = 0.7978845608028654
    square_gate = gate * gate
    turn = jnp.tanh(scale * (gate + 0.044715 * (square_gate * gate)))
    value = 0.5 * gate * (1.0 + turn)
    slope = 0.5 * (1.0 + turn) + 0.5 * gate * (1.0 - turn * turn) * (
        scale * (1.0 + 3.0 * 0.044715 * square_gate)
    )
    return value, slope


def shards(
    tokens,
    query_weight,
    key_weight,
    value_weight,
    output_weight,
    attn_norm,
    post_attn_norm,
    ffn_norm,
    post_ffn_norm,
    gate_weight,
    up_weight,
    down_weight,
    cotangent,
):
    size, width = tokens.shape
    seq_count = lax.axis_size("seq")
    dp_count = lax.axis_size("dp")
    heads = HQ // seq_count
    sharing = max(1, seq_count // HK)
    groups = [[first + i for i in range(sharing)] for first in range(0, seq_count, sharing)]
    kv_heads = max(1, HK // seq_count)
    copies = heads // kv_heads

    if sharing > 1:
        key_weight = lax.all_gather(
            key_weight, "seq", axis=1, tiled=True, axis_index_groups=groups
        )
        value_weight = lax.all_gather(
            value_weight, "seq", axis=1, tiled=True, axis_index_groups=groups
        )
    q_cols, kv_cols = heads * HD, kv_heads * HD
    hidden_units = gate_weight.shape[1]
    first_value = q_cols + kv_cols
    all_cols = first_value + kv_cols
    w_attn = gather_width(
        jnp.concatenate([query_weight, key_weight, value_weight, output_weight], axis=1)
    )
    w_qkv, w_output = w_attn[:, :all_cols], w_attn[:, all_cols:]
    w_ffn = gather_width(jnp.concatenate([gate_weight, up_weight], axis=1))
    w_down = gather_width(down_weight)

    stacked = jnp.stack([attn_norm, post_attn_norm, ffn_norm, post_ffn_norm])
    scales = gather_small(stacked, "dp").transpose(1, 0, 2).reshape(4, width)
    scales = 1.0 + scales.astype(WIDE)
    scale_one, scale_two, scale_three, scale_four = (scales[i : i + 1] for i in range(4))

    whole_tokens = gather_rows(tokens).astype(WIDE)
    normed = (whole_tokens * norm_factor(whole_tokens) * scale_one).astype(LOW)
    length = size * seq_count
    places = (chunk_places(seq_count)[:, None] * size + jnp.arange(size)[None, :]).reshape(length)
    half = HD // 2
    freqs = 10000.0 ** (-jnp.arange(half).astype(WIDE) / half)
    angles = places.astype(WIDE)[:, None] * freqs[None, :]
    cosine, sine = jnp.cos(angles), jnp.sin(angles)
    allowed = (places[None, :] <= places[:, None]) & (
        places[:, None] - places[None, :] < WINDOW
    )
    q_scale = HD ** (-0.5)
    linear = dot(normed, w_qkv)
    queries = [
        (rotate(linear[:, h * HD : (h + 1) * HD], cosine, sine) * q_scale).astype(LOW)
        for h in range(heads)
    ]
    keys = [
        rotate(linear[:, q_cols + j * HD : q_cols + (j + 1) * HD], cosine, sine).astype(LOW)
        for j in range(kv_heads)
    ]
    values = [
        linear[:, first_value + j * HD : first_value + (j + 1) * HD].astype(LOW)
        for j in range(kv_heads)
    ]
    probs, turns, head_outs = [], [], []
    for h in range(heads):
        turn = jnp.tanh(dot_last(queries[h], keys[h // copies]) / SOFT_CAP)
        capped = jnp.where(allowed, SOFT_CAP * turn, -1e30)
        highest = jnp.max(capped, axis=-1, keepdims=True)
        weights = jnp.exp(capped - highest)
        prob = weights / jnp.sum(weights, axis=-1, keepdims=True)
        probs.append(prob)
        turns.append(turn)
        head_outs.append(dot(prob.astype(LOW), values[h // copies]).astype(LOW))
    mixed = jnp.concatenate(head_outs, axis=1)
    projected = scatter_rows(lambda a, b: dot_last(mixed[a:b], w_output), size)

    inputs = tokens.astype(WIDE)
    factor_two = norm_factor(projected)
    hidden = inputs + projected * factor_two * scale_two
    factor_three = norm_factor(hidden)
    whole_in = gather_rows((hidden * factor_three * scale_three).astype(LOW))
    gate_up = dot(whole_in, w_ffn)
    gate, upward = gate_up[:, :hidden_units], gate_up[:, hidden_units:]
    activated, slope = gelu_parts(gate)
    inner = (activated * upward).astype(LOW)
    ffn_raw = scatter_rows(lambda a, b: dot_last(inner[a:b], w_down), size)
    factor_four = norm_factor(ffn_raw)
    result = (hidden + ffn_raw * factor_four * scale_four).astype(LOW)

    grad_result = cotangent.astype(WIDE)
    grad_raw, grad_scale_four = norm_back(ffn_raw, factor_four, scale_four, grad_result)
    whole_grad = gather_rows(grad_raw.astype(LOW))
    send_down, whole_grad = hold_first(dot_first(whole_grad, inner), whole_grad)
    grad_inner = dot(whole_grad, w_down)
    grad_ffn = jnp.concatenate(
        [(grad_inner * upward * slope).astype(LOW), (grad_inner * activated).astype(LOW)], axis=1
    )
    send_ffn, grad_ffn = hold_first(dot_first(whole_in, grad_ffn), grad_ffn)
    grad_ffn_in = scatter_rows(lambda a, b: dot_last(grad_ffn[a:b], w_ffn), size)
    back_three, grad_scale_three = norm_back(hidden, factor_three, scale_three, grad_ffn_in)
    grad_hidden = grad_result + back_three
    back_two, grad_scale_two = norm_back(projected, factor_two, scale_two, grad_hidden)
    whole_proj = gather_rows(back_two.astype(LOW))
    send_output, whole_proj = hold_first(dot_first(whole_proj, mixed), whole_proj)
    grad_mixed = dot(whole_proj, w_output).astype(LOW)

    grad_q, grad_k, grad_v = [], [0.0] * kv_heads, [0.0] * kv_heads
    for h in range(heads):
        j = h // copies
        grad_head = grad_mixed[:, h * HD : (h + 1) * HD]
        grad_probs = dot_last(grad_head, values[j])
        across = jnp.sum(grad_probs * probs[h], axis=-1, keepdims=True)
        grad_scores = (
            probs[h] * (grad_probs - across) * (1.0 - turns[h] * turns[h])
        ).astype(LOW)
        grad_q.append(
            (rotate(dot(grad_scores, keys[j]), cosine, -sine) * q_scale).astype(LOW)
        )
        grad_k[j] = grad_k[j] + dot_first(grad_scores, queries[h])
        grad_v[j] = grad_v[j] + dot_first(probs[h].astype(LOW), grad_head)
    grad_k = [rotate(item, cosine, -sine).astype(LOW) for item in grad_k]
    grad_v = [item.astype(LOW) for item in grad_v]
    grad_linear = jnp.concatenate(grad_q + grad_k + grad_v, axis=1)
    send_qkv, grad_linear = hold_first(dot_first(normed, grad_linear), grad_linear)
    grad_normed = scatter_rows(lambda a, b: dot_last(grad_linear[a:b], w_qkv), size)
    back_one, grad_scale_one = norm_back(inputs, norm_factor(inputs), scale_one, grad_normed)
    grad_tokens = grad_hidden + back_one

    shard_down, _ = scatter_width(send_down)
    shard_ffn, shard_down = scatter_width(send_ffn, shard_down)
    shard_output, shard_ffn = scatter_width(send_output, shard_ffn)
    shard_qkv, shard_output = scatter_width(send_qkv, shard_output)
    shard_down, shard_ffn, shard_output, shard_qkv = (
        item.astype(WIDE) for item in (shard_down, shard_ffn, shard_output, shard_qkv)
    )
    shard_gate, shard_up = shard_ffn[:, :hidden_units], shard_ffn[:, hidden_units:]
    shard_query = shard_qkv[:, :q_cols]
    shard_key = shard_qkv[:, q_cols:first_value]
    shard_value = shard_qkv[:, first_value:]
    if sharing > 1:
        shard_key, shard_value = (
            lax.psum_scatter(
                item.astype(LOW),
                "seq",
                scatter_dimension=1,
                tiled=True,
                axis_index_groups=groups,
            ).astype(WIDE)
            for item in (shard_key, shard_value)
        )

    piece = width // (dp_count * seq_count)
    stacked = jnp.stack([grad_scale_one, grad_scale_two, grad_scale_three, grad_scale_four])
    packed = stacked.reshape(4, dp_count, seq_count, piece).transpose(1, 2, 0, 3)
    packed = packed.reshape(dp_count, seq_count, 4 * piece)
    owned = scatter_small(scatter_small(packed, "dp"), "seq").reshape(4, piece)
    return (
        result,
        grad_tokens,
        shard_query,
        shard_key,
        shard_value,
        shard_output,
        owned[0],
        owned[1],
        owned[2],
        owned[3],
        shard_gate,
        shard_up,
        shard_down,
    )


def solution(mesh):
    rows = P(("dp", "seq"), None)
    weight = P("dp", "seq")
    scale = P("dp")
    scale_grad = P(("dp", "seq"))
    in_specs = (
        (rows,) + (weight,) * 4 + (scale,) * 4 + (weight,) * 3 + (rows,)
    )
    out_specs = (rows, rows) + (weight,) * 4 + (scale_grad,) * 4 + (weight,) * 3
    return jax.shard_map(
        shards, mesh=mesh, in_specs=in_specs, out_specs=out_specs, check_vma=False
    )
```

```python
import functools

import jax
import jax.numpy as jnp
from jax import lax
from jax.experimental import pallas as pl
from jax.experimental.pallas import tpu as pltpu
from jax.sharding import PartitionSpec as P

HQ = 8
HK = 4
HD = 256
WINDOW = 4096
EPSILON = 1e-06
SOFT_CAP = 50.0
LOW = jnp.bfloat16
WIDE = jnp.float32
VMEM_BYTES = 48 * 1024 * 1024


def swap_pairs(count, mask):
    return [(i, i ^ mask) for i in range(count)]


def gather_small(values, axis):
    count = lax.axis_size(axis)
    if count & (count - 1):
        return lax.all_gather(values, axis, axis=0, tiled=False)
    place = lax.axis_index(axis)
    held = values[None]
    bit = 1
    while bit < count:
        other = lax.ppermute(held, axis, swap_pairs(count, bit))
        upper = (place & bit) != 0
        held = jnp.where(
            upper, jnp.concatenate([other, held]), jnp.concatenate([held, other])
        )
        bit *= 2
    return held


def scatter_small(values, axis):
    count = lax.axis_size(axis)
    if count & (count - 1):
        return lax.psum_scatter(values, axis, scatter_dimension=0, tiled=False)
    place = lax.axis_index(axis)
    bit = count // 2
    while bit:
        halves = values.reshape((2, bit) + values.shape[1:])
        upper = (place & bit) != 0
        keep = jnp.where(upper, halves[1], halves[0])
        send = jnp.where(upper, halves[0], halves[1])
        values = keep + lax.ppermute(send, axis, swap_pairs(count, bit))
        bit //= 2
    return values[0]


def square(count):
    return count == 4


def chunk_places(count):
    here = lax.axis_index("seq")
    if square(count):
        return here ^ jnp.arange(count)
    return jnp.arange(count)


def gather_rows(rows, between=None):
    count = lax.axis_size("seq")
    if not square(count):
        if between is not None:
            (rows,) = between(rows)
        return lax.all_gather(rows, "seq", axis=0, tiled=True)
    half = rows.shape[0] // 2
    along, across = swap_pairs(count, 1), swap_pairs(count, 2)
    top, low = rows[:half], rows[half:]
    y_top = lax.ppermute(top, "seq", across)
    x_low = lax.ppermute(low, "seq", along)
    y_low = lax.ppermute(low, "seq", across)
    x_top = lax.ppermute(top, "seq", along)
    if between is not None:
        y_top, x_low = between(y_top, x_low)
    far_top = lax.ppermute(y_top, "seq", along)
    far_low = lax.ppermute(x_low, "seq", across)
    return jnp.concatenate([rows, x_top, x_low, y_top, y_low, far_top, far_low])


def scatter_rows(partial, size, sent=None):
    count = lax.axis_size("seq")
    if not square(count):
        rows = partial(0, count * size).astype(LOW)
        if sent is not None:
            sent(rows)
        return lax.psum_scatter(rows, "seq", scatter_dimension=0, tiled=True).astype(WIDE)
    half = size // 2
    along, across = swap_pairs(count, 1), swap_pairs(count, 2)
    far = partial(3 * size, 4 * size).astype(LOW)
    via_x = lax.ppermute(far[:half], "seq", along)
    via_y = lax.ppermute(far[half:], "seq", across)
    to_x = partial(size, 2 * size)
    x_top = lax.ppermute(to_x[:half].astype(LOW), "seq", along)
    to_y = partial(2 * size, 3 * size)
    y_low = lax.ppermute(to_y[half:].astype(LOW), "seq", across)
    x_low = (to_x[half:] + via_y.astype(WIDE)).astype(LOW)
    y_top = (to_y[:half] + via_x.astype(WIDE)).astype(LOW)
    if sent is not None:
        sent(x_low, y_top)
    x_low = lax.ppermute(x_low, "seq", along)
    y_top = lax.ppermute(y_top, "seq", across)
    own = partial(0, size)
    from_x = jnp.concatenate([x_top, x_low]).astype(WIDE)
    from_y = jnp.concatenate([y_top, y_low]).astype(WIDE)
    return own + from_x + from_y


def gather_width(shard):
    return lax.all_gather(shard, "dp", axis=0, tiled=True)


def line_pairs(first, last, step):
    return [(2 * i + c, 2 * (i + step) + c) for i in range(first, last + 1) for c in range(2)]


def core_pairs(planes):
    return swap_pairs(2 * planes, 1)


def row_block(rows):
    return next(size for size in (256, 128, 64, 32, 16) if rows % size == 0)


def split_kernel(block, core, rows, parts):
    values = rows[...].astype(WIDE)
    pieces = [values[:, i : i + block] for i in range(0, values.shape[1], block)]
    parts[core[0]] = jnp.concatenate(pieces[0::2], axis=1).astype(LOW)
    parts[1 - core[0]] = jnp.concatenate(pieces[1::2], axis=1).astype(LOW)


def by_core(rows):
    dp_count = lax.axis_size("dp")
    if dp_count % 2:
        return rows, None
    count, width = rows.shape
    size = row_block(count)
    parts = pl.pallas_call(
        functools.partial(split_kernel, width // dp_count),
        out_shape=jax.ShapeDtypeStruct((2, count, width // 2), LOW),
        grid=(count // size,),
        in_specs=[
            pl.BlockSpec(memory_space=pltpu.SMEM),
            pl.BlockSpec((size, width), lambda i: (i, 0)),
        ],
        out_specs=pl.BlockSpec((2, size, width // 2), lambda i: (0, i, 0)),
        compiler_params=pltpu.CompilerParams(vmem_limit_bytes=VMEM_BYTES),
        name="split_columns",
    )((lax.axis_index("dp") % 2).astype(jnp.int32).reshape(1), rows)
    return parts[0], parts[1]


def inner_kernel(rows, weight, slope, value, to_gate, to_up):
    grad = jnp.dot(rows[...], weight[...], preferred_element_type=WIDE)
    to_gate[...] = (grad * slope[...].astype(WIDE)).astype(LOW)
    to_up[...] = (grad * value[...].astype(WIDE)).astype(LOW)


def inner_back(rows, weight, slope, value):
    count, width = rows.shape
    units = weight.shape[1]
    size = 256 if units % 256 == 0 else 128
    part = pl.BlockSpec((count, size), lambda j: (0, j))
    shape = jax.ShapeDtypeStruct((count, units), LOW)
    return pl.pallas_call(
        inner_kernel,
        out_shape=[shape, shape],
        grid=(units // size,),
        in_specs=[
            pl.BlockSpec((count, width), lambda j: (0, 0)),
            pl.BlockSpec((width, size), lambda j: (0, j)),
            part,
            part,
        ],
        out_specs=[part, part],
        compiler_params=pltpu.CompilerParams(vmem_limit_bytes=VMEM_BYTES),
        cost_estimate=pl.CostEstimate(flops=0, bytes_accessed=0, transcendentals=0),
        name="inner_back",
    )(rows, weight, slope, value)


def product_kernel(left, right, *refs):
    total = jnp.dot(left[...], right[...], preferred_element_type=WIDE)
    if len(refs) == 2:
        total = total + refs[0][...].astype(WIDE)
    refs[-1][...] = total.astype(LOW)


def product(left, right, *more):
    rows, depth = left.shape
    columns = right.shape[1]
    size = 256 if columns % 256 == 0 else 128
    part = pl.BlockSpec((rows, size), lambda j: (0, j))
    return pl.pallas_call(
        product_kernel,
        out_shape=jax.ShapeDtypeStruct((rows, columns), LOW),
        grid=(columns // size,),
        in_specs=[
            pl.BlockSpec((rows, depth), lambda j: (0, 0)),
            pl.BlockSpec((depth, size), lambda j: (0, j)),
        ]
        + [part] * len(more),
        out_specs=part,
        compiler_params=pltpu.CompilerParams(vmem_limit_bytes=VMEM_BYTES),
        cost_estimate=pl.CostEstimate(flops=0, bytes_accessed=0, transcendentals=0),
        name="product",
    )(left, right, *more)


def attention_back_kernel(
    copies, q_scale, q, k, v, grad, probs, slopes, cosine, sine, out, grad_k, grad_v
):
    head, step = pl.program_id(0), pl.program_id(1)
    size, length = q.shape[0], k.shape[0]
    rows = pl.ds(pl.multiple_of(step * size, size), size)
    low = probs[0]
    grad_probs = dot_last(grad[...], v[...])
    across = jnp.sum(grad_probs * low.astype(WIDE), axis=-1, keepdims=True)
    grad_scores = (slopes[0].astype(WIDE) * (grad_probs - across)).astype(LOW)
    grad_q = rotate(dot(grad_scores, k[...]), cosine[rows, :], -sine[rows, :]) * q_scale
    out[rows, pl.ds(pl.multiple_of(head * HD, HD), HD)] = grad_q.astype(LOW)
    more_k = dot_first(grad_scores, q[...])
    more_v = dot_first(low, grad[...])
    first = (step == 0) & (head % copies == 0)

    @pl.when(first)
    def _():
        grad_k[...] = more_k
        grad_v[...] = more_v

    @pl.when(jnp.logical_not(first))
    def _():
        grad_k[...] += more_k
        grad_v[...] += more_v

    @pl.when((step == length // size - 1) & (head % copies == copies - 1))
    def _():
        heads = pl.num_programs(0)
        place = heads + head // copies
        to_k = pl.ds(pl.multiple_of(place * HD, HD), HD)
        to_v = pl.ds(pl.multiple_of((place + heads // copies) * HD, HD), HD)
        out[:, to_k] = rotate(grad_k[...], cosine[...], -sine[...]).astype(LOW)
        out[:, to_v] = grad_v[...].astype(LOW)


def attention_back(queries, keys, values, grad, probs, slopes, cosine, sine, q_scale):
    length, q_cols = queries.shape
    kv_cols = keys.shape[1]
    heads, copies = q_cols // HD, q_cols // kv_cols
    size = row_block(length)
    by_rows = pl.BlockSpec((size, HD), lambda h, i: (i, h))
    by_kv = pl.BlockSpec((length, HD), lambda h, i: (0, h // copies))
    scores = pl.BlockSpec((1, size, length), lambda h, i: (h, i, 0))
    angle = pl.BlockSpec((length, HD // 2), lambda h, i: (0, 0))
    columns = q_cols + 2 * kv_cols
    return pl.pallas_call(
        functools.partial(attention_back_kernel, copies, q_scale),
        out_shape=jax.ShapeDtypeStruct((length, columns), LOW),
        grid=(heads, length // size),
        in_specs=[by_rows, by_kv, by_kv, by_rows, scores, scores, angle, angle],
        out_specs=pl.BlockSpec((length, columns), lambda h, i: (0, 0)),
        scratch_shapes=[pltpu.VMEM((length, HD), WIDE)] * 2,
        compiler_params=pltpu.CompilerParams(vmem_limit_bytes=VMEM_BYTES),
        cost_estimate=pl.CostEstimate(flops=0, bytes_accessed=0, transcendentals=0),
        name="attention_back",
    )(queries, keys, values, grad, probs, slopes, cosine, sine)


def give_core(columns, right):
    if columns[1] is None:
        return None, None
    send = dot_first(columns[1], right).astype(LOW)
    return send, lax.ppermute(send, "dp", core_pairs(lax.axis_size("dp") // 2))


def core_sum(columns, right, got):
    total = dot_first(columns[0], right)
    if got is not None:
        total = total + got.astype(WIDE)
    return total.astype(LOW)


def plane_sum(both):
    count = lax.axis_size("dp")
    groups = None
    if count % 2 == 0:
        groups = [[2 * i + c for i in range(count // 2)] for c in range(2)]
    return lax.psum_scatter(
        both, "dp", scatter_dimension=0, tiled=True, axis_index_groups=groups
    )


def after(value, *before):
    return lax.optimization_barrier((value,) + before)


def gather_line(shard):
    count = lax.axis_size("dp")
    if count % 2:
        return gather_width(shard)
    planes = count // 2
    place = lax.axis_index("dp")
    plane, core = place // 2, place % 2
    risen = sunk = shard
    below, above = [], []
    for step in range(planes - 1):
        risen = lax.ppermute(risen, "dp", line_pairs(step, planes - 2, 1))
        sunk = lax.ppermute(sunk, "dp", line_pairs(1, planes - 1 - step, -1))
        below.insert(0, risen)
        above.append(sunk)
    held = jnp.stack(below + [shard] + above)
    held = lax.dynamic_slice_in_dim(held, planes - 1 - plane, planes, 0)
    other = lax.ppermute(held, "dp", core_pairs(planes))
    even = jnp.where(core == 0, held, other)
    odd = jnp.where(core == 0, other, held)
    return jnp.stack([even, odd], axis=1).reshape(count * shard.shape[0], shard.shape[1])


def dot(left, right):
    return jnp.dot(left, right, preferred_element_type=WIDE)


def dot_last(left, right):
    return lax.dot_general(left, right, (((1,), (1,)), ((), ())), preferred_element_type=WIDE)


def dot_first(left, right):
    return lax.dot_general(left, right, (((0,), (0,)), ((), ())), preferred_element_type=WIDE)


def norm_factor(values):
    return lax.rsqrt(jnp.mean(values * values, axis=-1, keepdims=True) + EPSILON)


def norm_back(values, factor, scale, grad):
    scaled = grad * scale
    inner = jnp.mean(scaled * values, axis=-1, keepdims=True)
    back = factor * scaled - values * (factor * factor * factor * inner)
    return back, jnp.sum(grad * values * factor, axis=0)


def rotate(values, cosine, sine):
    half = values.shape[1] // 2
    left = values[:, :half]
    right = values[:, half:]
    return jnp.concatenate([left * cosine - right * sine, right * cosine + left * sine], axis=1)


def gelu_parts(gate):
    scale = 0.7978845608028654
    square_gate = gate * gate
    turn = jnp.tanh(scale * (gate + 0.044715 * (square_gate * gate)))
    value = 0.5 * gate * (1.0 + turn)
    slope = 0.5 * (1.0 + turn) + 0.5 * gate * (1.0 - turn * turn) * (
        scale * (1.0 + 3.0 * 0.044715 * square_gate)
    )
    return value, slope


def shards(
    tokens,
    query_weight,
    key_weight,
    value_weight,
    output_weight,
    attn_norm,
    post_attn_norm,
    ffn_norm,
    post_ffn_norm,
    gate_weight,
    up_weight,
    down_weight,
    cotangent,
):
    size, width = tokens.shape
    seq_count = lax.axis_size("seq")
    dp_count = lax.axis_size("dp")
    heads = HQ // seq_count
    sharing = max(1, seq_count // HK)
    groups = [[first + i for i in range(sharing)] for first in range(0, seq_count, sharing)]
    kv_heads = max(1, HK // seq_count)
    copies = heads // kv_heads

    if sharing > 1:
        key_weight = lax.all_gather(
            key_weight, "seq", axis=1, tiled=True, axis_index_groups=groups
        )
        value_weight = lax.all_gather(
            value_weight, "seq", axis=1, tiled=True, axis_index_groups=groups
        )
    q_cols, kv_cols = heads * HD, kv_heads * HD
    hidden_units = gate_weight.shape[1]
    first_value = q_cols + kv_cols
    all_cols = first_value + kv_cols
    w_attn = gather_width(
        jnp.concatenate([query_weight, key_weight, value_weight, output_weight], axis=1)
    )
    w_qkv, w_output = w_attn[:, :all_cols], w_attn[:, all_cols:]
    w_ffn = gather_width(jnp.concatenate([gate_weight, up_weight], axis=1))
    w_down = gather_width(down_weight)

    stacked = jnp.stack([attn_norm, post_attn_norm, ffn_norm, post_ffn_norm])
    scales = gather_small(stacked, "dp").transpose(1, 0, 2).reshape(4, width)
    scales = 1.0 + scales.astype(WIDE)
    scale_one, scale_two, scale_three, scale_four = (scales[i : i + 1] for i in range(4))

    whole_tokens = gather_rows(tokens).astype(WIDE)
    normed = (whole_tokens * norm_factor(whole_tokens) * scale_one).astype(LOW)
    normed_cols = by_core(normed)
    length = size * seq_count
    places = (chunk_places(seq_count)[:, None] * size + jnp.arange(size)[None, :]).reshape(length)
    half = HD // 2
    freqs = 10000.0 ** (-jnp.arange(half).astype(WIDE) / half)
    angles = places.astype(WIDE)[:, None] * freqs[None, :]
    cosine, sine = jnp.cos(angles), jnp.sin(angles)
    allowed = (places[None, :] <= places[:, None]) & (
        places[:, None] - places[None, :] < WINDOW
    )
    q_scale = HD ** (-0.5)
    linear = dot(normed, w_qkv)
    parts = [linear[:, i * HD : (i + 1) * HD] for i in range(heads + 2 * kv_heads)]
    queries = [(rotate(part, cosine, sine) * q_scale).astype(LOW) for part in parts[:heads]]
    keys = [rotate(part, cosine, sine).astype(LOW) for part in parts[heads : heads + kv_heads]]
    values = [part.astype(LOW) for part in parts[heads + kv_heads :]]
    probs, slopes, head_outs = [], [], []
    for h in range(heads):
        turn = jnp.tanh(dot_last(queries[h], keys[h // copies]) / SOFT_CAP)
        capped = jnp.where(allowed, SOFT_CAP * turn, -1e30)
        highest = jnp.max(capped, axis=-1, keepdims=True)
        weights = jnp.exp(capped - highest)
        prob = weights / jnp.sum(weights, axis=-1, keepdims=True)
        probs.append(prob.astype(LOW))
        slopes.append((prob * (1.0 - turn * turn)).astype(LOW))
        head_outs.append(dot(probs[h], values[h // copies]).astype(LOW))
    probs, slopes = jnp.stack(probs), jnp.stack(slopes)
    queries, keys, values = (jnp.concatenate(item, axis=1) for item in (queries, keys, values))
    mixed = jnp.concatenate(head_outs, axis=1)
    mixed, queries, keys, values, probs, slopes = after(
        mixed, queries, keys, values, probs, slopes
    )
    projected = scatter_rows(lambda a, b: dot_last(mixed[a:b], w_output), size)

    inputs = tokens.astype(WIDE)
    factor_two = norm_factor(projected)
    hidden = inputs + projected * factor_two * scale_two
    factor_three = norm_factor(hidden)
    whole_in = gather_rows((hidden * factor_three * scale_three).astype(LOW))
    in_mine, in_other = by_core(whole_in)
    in_mine = in_mine.T
    in_other = None if in_other is None else in_other.T
    gate_up = dot(whole_in, w_ffn)
    gate, upward = gate_up[:, :hidden_units], gate_up[:, hidden_units:]
    activated, slope = gelu_parts(gate)
    inner = (activated * upward).astype(LOW)
    slope, activated = (slope * upward).astype(LOW), activated.astype(LOW)
    inner, slope, activated, in_mine, in_other = after(inner, slope, activated, in_mine, in_other)
    ffn_raw = scatter_rows(lambda a, b: dot_last(inner[a:b], w_down), size)
    factor_four = norm_factor(ffn_raw)
    result = (hidden + ffn_raw * factor_four * scale_four).astype(LOW)

    grad_result = cotangent.astype(WIDE)
    grad_raw, grad_scale_four = norm_back(ffn_raw, factor_four, scale_four, grad_result)
    whole_grad = gather_rows(grad_raw.astype(LOW))
    grad_cols = by_core(whole_grad)
    send, got = give_core(grad_cols, inner)
    _, grad_cols = after(send, grad_cols)
    sum_down = core_sum(grad_cols, inner, got)
    sum_down, whole_grad = after(sum_down, whole_grad)
    down_low = plane_sum(sum_down)
    grad_gate, grad_up = inner_back(whole_grad, w_down, slope, activated)
    swap = core_pairs(dp_count // 2)
    got_gate = got_up = ()
    if in_other is not None:
        send, grad_gate, grad_up = after(product(in_other, grad_gate), grad_gate, grad_up)
        got_gate = (lax.ppermute(send, "dp", swap),)
    gate_low = sum_up = None

    def ffn_in_sent(*rows):
        nonlocal grad_gate, grad_up, down_low, gate_low, got_up, sum_up
        late = after(grad_gate, *rows)[0]
        sum_gate = product(in_mine, late, *got_gate)
        sum_gate, grad_gate, grad_up, down_low = after(sum_gate, grad_gate, grad_up, down_low)
        gate_low = plane_sum(sum_gate)

    def ffn_in_rows(start, stop):
        return dot_last(grad_gate[start:stop], w_ffn[:, :hidden_units]) + dot_last(
            grad_up[start:stop], w_ffn[:, hidden_units:]
        )

    grad_ffn_in = scatter_rows(ffn_in_rows, size, ffn_in_sent)
    if in_other is not None:
        send, grad_up = after(product(in_other, grad_up), grad_up)
        got_up = (lax.ppermute(send, "dp", swap),)
    sum_up = product(in_mine, grad_up, *got_up)
    back_three, grad_scale_three = norm_back(hidden, factor_three, scale_three, grad_ffn_in)
    grad_hidden = grad_result + back_three
    back_two, grad_scale_two = norm_back(projected, factor_two, scale_two, grad_hidden)
    up_low = None

    def proj_between(*rows):
        nonlocal up_low
        held = after(sum_up, *rows)
        up_low = plane_sum(held[0])
        return held[1:]

    whole_proj = gather_rows(back_two.astype(LOW), proj_between)
    proj_cols = by_core(whole_proj)
    send, got_output = give_core(proj_cols, mixed)
    _, proj_cols = after(send, proj_cols)
    sum_output = core_sum(proj_cols, mixed, got_output)
    sum_output, whole_proj = after(sum_output, whole_proj)
    grad_mixed = dot(whole_proj, w_output).astype(LOW)

    grad_linear = attention_back(
        queries, keys, values, grad_mixed, probs, slopes, cosine, sine, q_scale
    )
    send, got = give_core(normed_cols, grad_linear)
    _, grad_linear = after(send, grad_linear)
    attn_low = None

    def normed_sent(*rows):
        nonlocal attn_low, gate_low, up_low
        sum_attn = jnp.concatenate([core_sum(normed_cols, grad_linear, got), sum_output], axis=1)
        sum_attn = after(sum_attn, *rows)[0]
        sum_attn, gate_low, up_low = after(sum_attn, gate_low, up_low)
        attn_low = plane_sum(sum_attn)

    grad_normed = scatter_rows(lambda a, b: dot_last(grad_linear[a:b], w_qkv), size, normed_sent)
    back_one, grad_scale_one = norm_back(inputs, norm_factor(inputs), scale_one, grad_normed)
    grad_tokens = grad_hidden + back_one

    shard_down, shard_gate, shard_up, shard_attn = (
        item.astype(WIDE) for item in (down_low, gate_low, up_low, attn_low)
    )
    shard_query = shard_attn[:, :q_cols]
    shard_output = shard_attn[:, all_cols:]
    shard_key = shard_attn[:, q_cols:first_value]
    shard_value = shard_attn[:, first_value:all_cols]
    if sharing > 1:
        shard_key, shard_value = (
            lax.psum_scatter(
                item.astype(LOW),
                "seq",
                scatter_dimension=1,
                tiled=True,
                axis_index_groups=groups,
            ).astype(WIDE)
            for item in (shard_key, shard_value)
        )

    piece = width // (dp_count * seq_count)
    stacked = jnp.stack([grad_scale_one, grad_scale_two, grad_scale_three, grad_scale_four])
    packed = stacked.reshape(4, dp_count, seq_count, piece).transpose(1, 2, 0, 3)
    packed = packed.reshape(dp_count, seq_count, 4 * piece)
    owned = scatter_small(scatter_small(packed, "dp"), "seq").reshape(4, piece)
    return (
        result,
        grad_tokens,
        shard_query,
        shard_key,
        shard_value,
        shard_output,
        owned[0],
        owned[1],
        owned[2],
        owned[3],
        shard_gate,
        shard_up,
        shard_down,
    )


def solution(mesh):
    rows = P(("dp", "seq"), None)
    weight = P("dp", "seq")
    scale = P("dp")
    scale_grad = P(("dp", "seq"))
    in_specs = (
        (rows,) + (weight,) * 4 + (scale,) * 4 + (weight,) * 3 + (rows,)
    )
    out_specs = (rows, rows) + (weight,) * 4 + (scale_grad,) * 4 + (weight,) * 3
    return jax.shard_map(
        shards, mesh=mesh, in_specs=in_specs, out_specs=out_specs, check_vma=False
    )
```

```python
import functools

import jax
import jax.numpy as jnp
from jax import lax
from jax.experimental import pallas as pl
from jax.experimental.pallas import tpu as pltpu
from jax.sharding import PartitionSpec as P

HQ = 8
HK = 4
HD = 256
WINDOW = 4096
EPSILON = 1e-06
SOFT_CAP = 50.0
LOW = jnp.bfloat16
WIDE = jnp.float32
VMEM_BYTES = 48 * 1024 * 1024


def swap_pairs(count, mask):
    return [(i, i ^ mask) for i in range(count)]


def gather_small(values, axis):
    count = lax.axis_size(axis)
    if count & (count - 1):
        return lax.all_gather(values, axis, axis=0, tiled=False)
    place = lax.axis_index(axis)
    held = values[None]
    bit = 1
    while bit < count:
        other = lax.ppermute(held, axis, swap_pairs(count, bit))
        upper = (place & bit) != 0
        held = jnp.where(
            upper, jnp.concatenate([other, held]), jnp.concatenate([held, other])
        )
        bit *= 2
    return held


def scatter_small(values, axis):
    count = lax.axis_size(axis)
    if count & (count - 1):
        return lax.psum_scatter(values, axis, scatter_dimension=0, tiled=False)
    place = lax.axis_index(axis)
    bit = count // 2
    while bit:
        halves = values.reshape((2, bit) + values.shape[1:])
        upper = (place & bit) != 0
        keep = jnp.where(upper, halves[1], halves[0])
        send = jnp.where(upper, halves[0], halves[1])
        values = keep + lax.ppermute(send, axis, swap_pairs(count, bit))
        bit //= 2
    return values[0]


def square(count):
    return count == 4


def chunk_places(count):
    here = lax.axis_index("seq")
    if square(count):
        return here ^ jnp.arange(count)
    return jnp.arange(count)


def gather_rows(rows, between=None, halves=False):
    count = lax.axis_size("seq")
    if not square(count):
        if between is not None:
            (rows,) = between(rows)
        rows = lax.all_gather(rows, "seq", axis=0, tiled=not halves)
        if halves:
            rows = rows.reshape(count, 2, -1, rows.shape[2]).transpose(1, 0, 2, 3)
            rows = rows.reshape(-1, rows.shape[3])
        return rows
    half = rows.shape[0] // 2
    along, across = swap_pairs(count, 1), swap_pairs(count, 2)
    top, low = rows[:half], rows[half:]
    y_top = lax.ppermute(top, "seq", across)
    x_low = lax.ppermute(low, "seq", along)
    y_low = lax.ppermute(low, "seq", across)
    x_top = lax.ppermute(top, "seq", along)
    if between is not None:
        y_top, x_low = between(y_top, x_low)
    far_top = lax.ppermute(y_top, "seq", along)
    far_low = lax.ppermute(x_low, "seq", across)
    if halves:
        return jnp.concatenate([top, x_top, y_top, far_top, low, x_low, y_low, far_low])
    return jnp.concatenate([rows, x_top, x_low, y_top, y_low, far_top, far_low])


def scatter_rows(partial, size, early=None, sent=None):
    count = lax.axis_size("seq")
    if not square(count):
        rows = partial(0, count * size).astype(LOW)
        if early is not None:
            (rows,) = early(rows)
        if sent is not None:
            sent(rows)
        return lax.psum_scatter(rows, "seq", scatter_dimension=0, tiled=True).astype(WIDE)
    half = size // 2
    along, across = swap_pairs(count, 1), swap_pairs(count, 2)
    far = partial(3 * size, 4 * size).astype(LOW)
    via_x = lax.ppermute(far[:half], "seq", along)
    via_y = lax.ppermute(far[half:], "seq", across)
    to_both = partial(size, 3 * size)
    to_x, to_y = to_both[:size], to_both[size:]
    x_top = lax.ppermute(to_x[:half].astype(LOW), "seq", along)
    y_low = lax.ppermute(to_y[half:].astype(LOW), "seq", across)
    if early is not None:
        to_x, to_y = early(to_x, to_y)
    x_low = (to_x[half:] + via_y.astype(WIDE)).astype(LOW)
    y_top = (to_y[:half] + via_x.astype(WIDE)).astype(LOW)
    if sent is not None:
        sent(x_low, y_top)
    x_low = lax.ppermute(x_low, "seq", along)
    y_top = lax.ppermute(y_top, "seq", across)
    own = lax.optimization_barrier(partial(0, size))
    from_x = jnp.concatenate([x_top, x_low]).astype(WIDE)
    from_y = jnp.concatenate([y_top, y_low]).astype(WIDE)
    return own + from_x + from_y


def gather_width(shard):
    return lax.all_gather(shard, "dp", axis=0, tiled=True)


def line_pairs(first, last, step):
    return [(2 * i + c, 2 * (i + step) + c) for i in range(first, last + 1) for c in range(2)]


def core_pairs(planes):
    return swap_pairs(2 * planes, 1)


def row_block(rows):
    return next(size for size in (256, 128, 64, 32, 16) if rows % size == 0)


def column_block(columns):
    return next(size for size in (768, 512, 384, 256, 128) if columns % size == 0)


def this_core():
    return (lax.axis_index("dp") % 2).astype(jnp.int32).reshape(1)


def split_kernel(block, core, rows, parts):
    values = rows[...].astype(WIDE)
    pieces = [values[:, i : i + block] for i in range(0, values.shape[1], block)]
    even = jnp.concatenate(pieces[0::2], axis=1).astype(LOW)
    odd = jnp.concatenate(pieces[1::2], axis=1).astype(LOW)
    half = even.shape[1]

    @pl.when(core[0] == 0)
    def _():
        parts[:, :half] = even
        parts[:, half:] = odd

    @pl.when(core[0] != 0)
    def _():
        parts[:, :half] = odd
        parts[:, half:] = even


def by_core(rows):
    count, width = rows.shape
    size = row_block(count)
    whole = pl.BlockSpec((size, width), lambda i: (i, 0))
    return pl.pallas_call(
        functools.partial(split_kernel, width // lax.axis_size("dp")),
        out_shape=jax.ShapeDtypeStruct((count, width), LOW),
        grid=(count // size,),
        in_specs=[pl.BlockSpec(memory_space=pltpu.SMEM), whole],
        out_specs=whole,
        compiler_params=pltpu.CompilerParams(vmem_limit_bytes=VMEM_BYTES),
        name="split_columns",
    )(this_core(), rows)


def inner_kernel(block, late, core, mine, other, w_late, w_early, slope, value, to_gate, to_up):
    def go(weight):
        def part(rows, place):
            order = [2 * i + place for i in range(weight.shape[0] // block // 2)]
            blocks = [weight[pl.ds(pl.multiple_of(i * block, block), block), :] for i in order]
            return jnp.dot(rows[...], jnp.concatenate(blocks), preferred_element_type=WIDE)

        grad = part(mine, core[0]) + part(other, 1 - core[0])
        to_gate[...] = (grad * slope[...].astype(WIDE)).astype(LOW)
        to_up[...] = (grad * value[...].astype(WIDE)).astype(LOW)

    step = pl.program_id(0)
    pl.when(step < late)(lambda: go(w_late))
    pl.when(step >= late)(lambda: go(w_early))


def inner_back(mine, other, w_late, w_early, slope, value):
    count, half = other.shape
    width = 2 * half
    units = slope.shape[1]
    size = 256 if w_late.shape[1] % 256 == 0 and w_early.shape[1] % 256 == 0 else 128
    late = w_late.shape[1] // size
    part = pl.BlockSpec((count, size), lambda j: (0, j))
    shape = jax.ShapeDtypeStruct((count, units), LOW)
    return pl.pallas_call(
        functools.partial(inner_kernel, width // lax.axis_size("dp"), late),
        out_shape=[shape, shape],
        grid=(units // size,),
        in_specs=[
            pl.BlockSpec(memory_space=pltpu.SMEM),
            pl.BlockSpec((count, half), lambda j: (0, 0)),
            pl.BlockSpec((count, half), lambda j: (0, 0)),
            pl.BlockSpec((width, size), lambda j: (0, jnp.minimum(j, late - 1))),
            pl.BlockSpec((width, size), lambda j: (0, jnp.maximum(j - late, 0))),
            part,
            part,
        ],
        out_specs=[part, part],
        compiler_params=pltpu.CompilerParams(vmem_limit_bytes=VMEM_BYTES),
        cost_estimate=pl.CostEstimate(flops=0, bytes_accessed=0, transcendentals=0),
        name="inner_back",
    )(this_core(), mine, other, w_late, w_early, slope, value)


def first_kernel(left, right, more, out, turned):
    @pl.when(pl.program_id(0) == 0)
    def _():
        turned[...] = left[...].T

    total = jnp.dot(turned[...], right[...], preferred_element_type=WIDE)
    out[...] = (total + more[...].astype(WIDE)).astype(LOW)


def product_first(left, right, more):
    depth, rows = left.shape[0], left.shape[1] // 2
    columns = right.shape[1]
    size = column_block(columns)
    part = pl.BlockSpec((rows, size), lambda j: (0, j))
    return pl.pallas_call(
        first_kernel,
        out_shape=jax.ShapeDtypeStruct((rows, columns), LOW),
        grid=(columns // size,),
        in_specs=[
            pl.BlockSpec((depth, rows), lambda j: (0, 0)),
            pl.BlockSpec((depth, size), lambda j: (0, j)),
            part,
        ],
        out_specs=part,
        scratch_shapes=[pltpu.VMEM((rows, depth), LOW)],
        compiler_params=pltpu.CompilerParams(vmem_limit_bytes=VMEM_BYTES),
        cost_estimate=pl.CostEstimate(flops=0, bytes_accessed=0, transcendentals=0),
        name="product_first",
    )(left, right, more)


def product_kernel(left, right, *refs):
    total = jnp.dot(left[...], right[...], preferred_element_type=WIDE)
    if len(refs) == 2:
        total = total + refs[0][...].astype(WIDE)
    refs[-1][...] = total.astype(LOW)


def product(left, right, *more):
    rows, depth = left.shape
    columns = right.shape[1]
    size = column_block(columns)
    part = pl.BlockSpec((rows, size), lambda j: (0, j))
    return pl.pallas_call(
        product_kernel,
        out_shape=jax.ShapeDtypeStruct((rows, columns), LOW),
        grid=(columns // size,),
        in_specs=[
            pl.BlockSpec((rows, depth), lambda j: (0, 0)),
            pl.BlockSpec((depth, size), lambda j: (0, j)),
        ]
        + [part] * len(more),
        out_specs=part,
        compiler_params=pltpu.CompilerParams(vmem_limit_bytes=VMEM_BYTES),
        cost_estimate=pl.CostEstimate(flops=0, bytes_accessed=0, transcendentals=0),
        name="product",
    )(left, right, *more)


def attention_back_kernel(
    copies, q_scale, q, k, v, grad, probs, slopes, cosine, sine, out, grad_k, grad_v
):
    head, step = pl.program_id(0), pl.program_id(1)
    size, length = q.shape[0], k.shape[0]
    rows = pl.ds(pl.multiple_of(step * size, size), size)
    low = probs[0]
    grad_probs = dot_last(grad[...], v[...])
    across = jnp.sum(grad_probs * low.astype(WIDE), axis=-1, keepdims=True)
    grad_scores = (slopes[0].astype(WIDE) * (grad_probs - across)).astype(LOW)
    grad_q = rotate(dot(grad_scores, k[...]), cosine[rows, :], -sine[rows, :]) * q_scale
    out[rows, pl.ds(pl.multiple_of(head * HD, HD), HD)] = grad_q.astype(LOW)
    more_k = dot_first(grad_scores, q[...])
    more_v = dot_first(low, grad[...])
    first = (step == 0) & (head % copies == 0)

    @pl.when(first)
    def _():
        grad_k[...] = more_k
        grad_v[...] = more_v

    @pl.when(jnp.logical_not(first))
    def _():
        grad_k[...] += more_k
        grad_v[...] += more_v

    @pl.when((step == length // size - 1) & (head % copies == copies - 1))
    def _():
        heads = pl.num_programs(0)
        place = heads + head // copies
        to_k = pl.ds(pl.multiple_of(place * HD, HD), HD)
        to_v = pl.ds(pl.multiple_of((place + heads // copies) * HD, HD), HD)
        out[:, to_k] = rotate(grad_k[...], cosine[...], -sine[...]).astype(LOW)
        out[:, to_v] = grad_v[...].astype(LOW)


def attention_back(queries, keys, values, grad, probs, slopes, cosine, sine, q_scale):
    length, q_cols = queries.shape
    kv_cols = keys.shape[1]
    heads, copies = q_cols // HD, q_cols // kv_cols
    size = row_block(length)
    by_rows = pl.BlockSpec((size, HD), lambda h, i: (i, h))
    by_kv = pl.BlockSpec((length, HD), lambda h, i: (0, h // copies))
    scores = pl.BlockSpec((1, size, length), lambda h, i: (h, i, 0))
    angle = pl.BlockSpec((length, HD // 2), lambda h, i: (0, 0))
    columns = q_cols + 2 * kv_cols
    return pl.pallas_call(
        functools.partial(attention_back_kernel, copies, q_scale),
        out_shape=jax.ShapeDtypeStruct((length, columns), LOW),
        grid=(heads, length // size),
        in_specs=[by_rows, by_kv, by_kv, by_rows, scores, scores, angle, angle],
        out_specs=pl.BlockSpec((length, columns), lambda h, i: (0, 0)),
        scratch_shapes=[pltpu.VMEM((length, HD), WIDE)] * 2,
        compiler_params=pltpu.CompilerParams(vmem_limit_bytes=VMEM_BYTES),
        cost_estimate=pl.CostEstimate(flops=0, bytes_accessed=0, transcendentals=0),
        name="attention_back",
    )(queries, keys, values, grad, probs, slopes, cosine, sine)


def swap_cores(values):
    return lax.ppermute(values, "dp", core_pairs(lax.axis_size("dp") // 2))


def other_half(columns):
    return columns[:, columns.shape[1] // 2 :]


def give_core(columns, right):
    send = dot_first(other_half(columns), right).astype(LOW)
    send, columns = after(send, columns)
    return swap_cores(send), columns


def plane_sum(both):
    planes = lax.axis_size("dp") // 2
    groups = [[2 * i + c for i in range(planes)] for c in range(2)]
    return lax.psum_scatter(
        both, "dp", scatter_dimension=0, tiled=True, axis_index_groups=groups
    )


def after(value, *before):
    return lax.optimization_barrier((value,) + before)


class LineGather:
    def __init__(self, shard):
        self.planes = lax.axis_size("dp") // 2
        self.shard = self.risen = self.sunk = shard
        self.below, self.above = [], []

    def advance(self, *before):
        step, last = len(self.below), self.planes - 1
        if step == last:
            return
        risen, sunk = after(self.risen, self.sunk, *before)[:2]
        self.risen = lax.ppermute(risen, "dp", line_pairs(step, last - 1, 1))
        self.sunk = lax.ppermute(sunk, "dp", line_pairs(1, last - step, -1))
        self.below.insert(0, self.risen)
        self.above.append(self.sunk)

    def whole(self):
        for _ in range(self.planes - 1):
            self.advance()
        place = lax.axis_index("dp")
        plane, core = place // 2, place % 2
        held = jnp.stack(self.below + [self.shard] + self.above)
        held = lax.dynamic_slice_in_dim(held, self.planes - 1 - plane, self.planes, 0)
        other = swap_cores(held)
        even = jnp.where(core == 0, held, other)
        odd = jnp.where(core == 0, other, held)
        rows = 2 * self.planes * self.shard.shape[0]
        return jnp.stack([even, odd], axis=1).reshape(rows, self.shard.shape[1])


def dot(left, right):
    return jnp.dot(left, right, preferred_element_type=WIDE)


def dot_last(left, right):
    return lax.dot_general(left, right, (((1,), (1,)), ((), ())), preferred_element_type=WIDE)


def dot_first(left, right):
    return lax.dot_general(left, right, (((0,), (0,)), ((), ())), preferred_element_type=WIDE)


def norm_factor(values):
    return lax.rsqrt(jnp.mean(values * values, axis=-1, keepdims=True) + EPSILON)


def norm_back(values, factor, scale, grad):
    scaled = grad * scale
    inner = jnp.mean(scaled * values, axis=-1, keepdims=True)
    back = factor * scaled - values * (factor * factor * factor * inner)
    return back, jnp.sum(grad * values * factor, axis=0)


def rotate(values, cosine, sine):
    half = values.shape[1] // 2
    left = values[:, :half]
    right = values[:, half:]
    return jnp.concatenate([left * cosine - right * sine, right * cosine + left * sine], axis=1)


def gelu_parts(gate):
    scale = 0.7978845608028654
    square_gate = gate * gate
    turn = jnp.tanh(scale * (gate + 0.044715 * (square_gate * gate)))
    value = 0.5 * gate * (1.0 + turn)
    slope = 0.5 * (1.0 + turn) + 0.5 * gate * (1.0 - turn * turn) * (
        scale * (1.0 + 3.0 * 0.044715 * square_gate)
    )
    return value, slope


def shards(
    tokens,
    query_weight,
    key_weight,
    value_weight,
    output_weight,
    attn_norm,
    post_attn_norm,
    ffn_norm,
    post_ffn_norm,
    gate_weight,
    up_weight,
    down_weight,
    cotangent,
):
    size, width = tokens.shape
    seq_count = lax.axis_size("seq")
    dp_count = lax.axis_size("dp")
    heads = HQ // seq_count
    sharing = max(1, seq_count // HK)
    groups = [[first + i for i in range(sharing)] for first in range(0, seq_count, sharing)]
    kv_heads = max(1, HK // seq_count)
    copies = heads // kv_heads

    if sharing > 1:
        key_weight = lax.all_gather(
            key_weight, "seq", axis=1, tiled=True, axis_index_groups=groups
        )
        value_weight = lax.all_gather(
            value_weight, "seq", axis=1, tiled=True, axis_index_groups=groups
        )
    q_cols, kv_cols = heads * HD, kv_heads * HD
    hidden_units = gate_weight.shape[1]
    first_value = q_cols + kv_cols
    all_cols = first_value + kv_cols
    w_attn = gather_width(
        jnp.concatenate([query_weight, key_weight, value_weight, output_weight], axis=1)
    )
    w_ffn = gather_width(jnp.concatenate([gate_weight, up_weight], axis=1))
    late = hidden_units - hidden_units * 5 // 9 // 128 * 128
    w_late = gather_width(down_weight[:, :late])
    w_qkv, w_output = w_attn[:, :all_cols], w_attn[:, all_cols:]

    stacked = jnp.stack([attn_norm, post_attn_norm, ffn_norm, post_ffn_norm])
    scales = gather_small(stacked, "dp").transpose(1, 0, 2).reshape(4, width)
    early_shard, scales = after(down_weight[:, late:], scales)
    line = LineGather(early_shard)
    line.advance()
    line.advance()
    scales = 1.0 + scales.astype(WIDE)
    scale_one, scale_two, scale_three, scale_four = (scales[i : i + 1] for i in range(4))

    whole_tokens = gather_rows(tokens).astype(WIDE)
    normed = (whole_tokens * norm_factor(whole_tokens) * scale_one).astype(LOW)
    normed_cols = by_core(normed)
    length = size * seq_count
    places = (chunk_places(seq_count)[:, None] * size + jnp.arange(size)[None, :]).reshape(length)
    half = HD // 2
    freqs = 10000.0 ** (-jnp.arange(half).astype(WIDE) / half)
    angles = places.astype(WIDE)[:, None] * freqs[None, :]
    cosine, sine = jnp.cos(angles), jnp.sin(angles)
    allowed = (places[None, :] <= places[:, None]) & (
        places[:, None] - places[None, :] < WINDOW
    )
    q_scale = HD ** (-0.5)
    linear = dot(normed, w_qkv)
    parts = [linear[:, i * HD : (i + 1) * HD] for i in range(heads + 2 * kv_heads)]
    queries = [(rotate(part, cosine, sine) * q_scale).astype(LOW) for part in parts[:heads]]
    keys = [rotate(part, cosine, sine).astype(LOW) for part in parts[heads : heads + kv_heads]]
    values = [part.astype(LOW) for part in parts[heads + kv_heads :]]
    probs, slopes, head_outs = [], [], []
    for h in range(heads):
        turn = jnp.tanh(dot_last(queries[h], keys[h // copies]) / SOFT_CAP)
        capped = jnp.where(allowed, SOFT_CAP * turn, -1e30)
        highest = jnp.max(capped, axis=-1, keepdims=True)
        weights = jnp.exp(capped - highest)
        prob = weights / jnp.sum(weights, axis=-1, keepdims=True)
        probs.append(prob.astype(LOW))
        slopes.append((prob * (1.0 - turn * turn)).astype(LOW))
        head_outs.append(dot(probs[h], values[h // copies]).astype(LOW))
    probs, slopes = jnp.stack(probs), jnp.stack(slopes)
    queries, keys, values = (jnp.concatenate(item, axis=1) for item in (queries, keys, values))
    mixed = jnp.concatenate(head_outs, axis=1)
    mixed, queries, keys, values, probs, slopes = after(
        mixed, queries, keys, values, probs, slopes
    )
    line.advance(mixed)
    w_early = line.whole()
    projected = scatter_rows(lambda a, b: dot_last(mixed[a:b], w_output), size)

    inputs = tokens.astype(WIDE)
    factor_two = norm_factor(projected)
    hidden = inputs + projected * factor_two * scale_two
    factor_three = norm_factor(hidden)
    whole_in = gather_rows((hidden * factor_three * scale_three).astype(LOW))
    gate_up = lax.optimization_barrier(dot(whole_in, w_ffn).astype(LOW))
    gate, upward = gate_up[:, :hidden_units].astype(WIDE), gate_up[:, hidden_units:].astype(WIDE)
    activated, slope = gelu_parts(gate)
    inner = (activated * upward).astype(LOW)
    slope, activated = (slope * upward).astype(LOW), activated.astype(LOW)
    inner, slope, activated = after(inner, slope, activated)
    in_cols = by_core(whole_in)
    in_mine, in_other = in_cols[:, : width // 2].T, other_half(in_cols).T
    in_mine, in_other, inner = after(in_mine, in_other, inner)
    early_raw = lax.optimization_barrier(dot_last(inner[:, late:], w_early))
    given = swap_cores(inner)
    ffn_raw = scatter_rows(
        lambda a, b: early_raw[a:b] + dot_last(inner[a:b, :late], w_late), size
    )
    factor_four = norm_factor(ffn_raw)
    result = (hidden + ffn_raw * factor_four * scale_four).astype(LOW)

    grad_result = cotangent.astype(WIDE)
    grad_raw, grad_scale_four = norm_back(ffn_raw, factor_four, scale_four, grad_result)
    grad_cols = by_core(grad_raw.astype(LOW))
    half = width // 2
    both_grad = gather_rows(
        jnp.concatenate([grad_cols[:, :half], swap_cores(other_half(grad_cols))]), halves=True
    )
    sum_down = dot_first(both_grad[:length], inner) + dot_first(both_grad[length:], given)
    sum_down = sum_down.astype(LOW)
    sum_down, both_grad = after(sum_down, both_grad)
    grad_other = swap_cores(both_grad[length:])
    down_low = plane_sum(sum_down)
    grad_gate, grad_up = inner_back(both_grad, grad_other, w_late, w_early, slope, activated)
    send, grad_gate, grad_up = after(product(in_other, grad_gate), grad_gate, grad_up)
    got_gate = swap_cores(send)
    gate_low = None

    def ffn_in_early(*rows):
        nonlocal grad_gate, grad_up, down_low, gate_low
        held = after(grad_gate, *rows)
        sum_gate = product(in_mine, held[0], got_gate)
        held = after(sum_gate, *held[1:])
        sum_gate, grad_gate, grad_up, down_low = after(held[0], grad_gate, grad_up, down_low)
        gate_low = plane_sum(sum_gate)
        return held[1:]

    def ffn_in_rows(start, stop):
        return dot_last(grad_gate[start:stop], w_ffn[:, :hidden_units]) + dot_last(
            grad_up[start:stop], w_ffn[:, hidden_units:]
        )

    grad_ffn_in = scatter_rows(ffn_in_rows, size, ffn_in_early)
    send, grad_up = after(product(in_other, grad_up), grad_up)
    sum_up = product(in_mine, grad_up, swap_cores(send))
    back_three, grad_scale_three = norm_back(hidden, factor_three, scale_three, grad_ffn_in)
    grad_hidden = grad_result + back_three
    back_two, grad_scale_two = norm_back(projected, factor_two, scale_two, grad_hidden)
    up_low = None

    def proj_between(*rows):
        nonlocal up_low
        held = after(sum_up, *rows)
        up_low = plane_sum(held[0])
        return held[1:]

    whole_proj = gather_rows(back_two.astype(LOW), proj_between)
    got, proj_cols = give_core(by_core(whole_proj), mixed)
    sum_output = product_first(proj_cols, mixed, got)
    sum_output, whole_proj = after(sum_output, whole_proj)
    grad_mixed = dot(whole_proj, w_output).astype(LOW)

    grad_linear = attention_back(
        queries, keys, values, grad_mixed, probs, slopes, cosine, sine, q_scale
    )
    got, normed_cols = give_core(normed_cols, grad_linear)
    attn_low = None

    def normed_sent(*rows):
        nonlocal attn_low, gate_low, up_low
        sum_attn = product_first(normed_cols, grad_linear, got)
        sum_attn = jnp.concatenate([sum_attn, sum_output], axis=1)
        sum_attn = after(sum_attn, *rows)[0]
        sum_attn, gate_low, up_low = after(sum_attn, gate_low, up_low)
        attn_low = plane_sum(sum_attn)

    grad_normed = scatter_rows(lambda a, b: dot_last(grad_linear[a:b], w_qkv), size, sent=normed_sent)
    back_one, grad_scale_one = norm_back(inputs, norm_factor(inputs), scale_one, grad_normed)
    grad_tokens = grad_hidden + back_one

    shard_down, shard_gate, shard_up, shard_attn = (
        item.astype(WIDE) for item in (down_low, gate_low, up_low, attn_low)
    )
    shard_query = shard_attn[:, :q_cols]
    shard_output = shard_attn[:, all_cols:]
    shard_key = shard_attn[:, q_cols:first_value]
    shard_value = shard_attn[:, first_value:all_cols]
    if sharing > 1:
        shard_key, shard_value = (
            lax.psum_scatter(
                item.astype(LOW),
                "seq",
                scatter_dimension=1,
                tiled=True,
                axis_index_groups=groups,
            ).astype(WIDE)
            for item in (shard_key, shard_value)
        )

    piece = width // (dp_count * seq_count)
    stacked = jnp.stack([grad_scale_one, grad_scale_two, grad_scale_three, grad_scale_four])
    packed = stacked.reshape(4, dp_count, seq_count, piece).transpose(1, 2, 0, 3)
    packed = packed.reshape(dp_count, seq_count, 4 * piece)
    owned = scatter_small(scatter_small(packed, "dp"), "seq").reshape(4, piece)
    return (
        result,
        grad_tokens,
        shard_query,
        shard_key,
        shard_value,
        shard_output,
        owned[0],
        owned[1],
        owned[2],
        owned[3],
        shard_gate,
        shard_up,
        shard_down,
    )


def solution(mesh):
    rows = P(("dp", "seq"), None)
    weight = P("dp", "seq")
    scale = P("dp")
    scale_grad = P(("dp", "seq"))
    in_specs = (
        (rows,) + (weight,) * 4 + (scale,) * 4 + (weight,) * 3 + (rows,)
    )
    out_specs = (rows, rows) + (weight,) * 4 + (scale_grad,) * 4 + (weight,) * 3
    return jax.shard_map(
        shards, mesh=mesh, in_specs=in_specs, out_specs=out_specs, check_vma=False
    )
```

```python
import functools

import jax
import jax.numpy as jnp
from jax import lax
from jax.experimental import pallas as pl
from jax.experimental.pallas import tpu as pltpu
from jax.sharding import PartitionSpec as P

HQ = 8
HK = 4
HD = 256
WINDOW = 4096
EPSILON = 1e-06
SOFT_CAP = 50.0
LOW = jnp.bfloat16
WIDE = jnp.float32
VMEM_BYTES = 48 * 1024 * 1024


def swap_pairs(count, mask):
    return [(i, i ^ mask) for i in range(count)]


def gather_small(values, axis):
    count = lax.axis_size(axis)
    if count & (count - 1):
        return lax.all_gather(values, axis, axis=0, tiled=False)
    place = lax.axis_index(axis)
    held = values[None]
    bit = 1
    while bit < count:
        other = lax.ppermute(held, axis, swap_pairs(count, bit))
        upper = (place & bit) != 0
        held = jnp.where(
            upper, jnp.concatenate([other, held]), jnp.concatenate([held, other])
        )
        bit *= 2
    return held


def scatter_small(values, axis):
    count = lax.axis_size(axis)
    if count & (count - 1):
        return lax.psum_scatter(values, axis, scatter_dimension=0, tiled=False)
    place = lax.axis_index(axis)
    bit = count // 2
    while bit:
        halves = values.reshape((2, bit) + values.shape[1:])
        upper = (place & bit) != 0
        keep = jnp.where(upper, halves[1], halves[0])
        send = jnp.where(upper, halves[0], halves[1])
        values = keep + lax.ppermute(send, axis, swap_pairs(count, bit))
        bit //= 2
    return values[0]


def square(count):
    return count == 4


def chunk_places(count):
    here = lax.axis_index("seq")
    if square(count):
        return here ^ jnp.arange(count)
    return jnp.arange(count)


def gather_rows(rows, between=None, halves=False):
    count = lax.axis_size("seq")
    if not square(count):
        if between is not None:
            (rows,) = between(rows)
        rows = lax.all_gather(rows, "seq", axis=0, tiled=not halves)
        if halves:
            rows = rows.reshape(count, 2, -1, rows.shape[2]).transpose(1, 0, 2, 3)
            rows = rows.reshape(-1, rows.shape[3])
        return rows
    half = rows.shape[0] // 2
    along, across = swap_pairs(count, 1), swap_pairs(count, 2)
    top, low = rows[:half], rows[half:]
    y_top = lax.ppermute(top, "seq", across)
    x_low = lax.ppermute(low, "seq", along)
    y_low = lax.ppermute(low, "seq", across)
    x_top = lax.ppermute(top, "seq", along)
    if between is not None:
        y_top, x_low = between(y_top, x_low)
    far_top = lax.ppermute(y_top, "seq", along)
    far_low = lax.ppermute(x_low, "seq", across)
    if halves:
        return jnp.concatenate([top, x_top, y_top, far_top, low, x_low, y_low, far_low])
    return jnp.concatenate([rows, x_top, x_low, y_top, y_low, far_top, far_low])


def scatter_rows(partial, size, early=None, sent=None):
    count = lax.axis_size("seq")
    if not square(count):
        rows = partial(0, count * size).astype(LOW)
        if early is not None:
            (rows,) = early(rows)
        if sent is not None:
            sent(rows)
        return lax.psum_scatter(rows, "seq", scatter_dimension=0, tiled=True).astype(WIDE)
    half = size // 2
    along, across = swap_pairs(count, 1), swap_pairs(count, 2)
    far = partial(3 * size, 4 * size).astype(LOW)
    via_x = lax.ppermute(far[:half], "seq", along)
    via_y = lax.ppermute(far[half:], "seq", across)
    to_both = partial(size, 3 * size)
    to_x, to_y = to_both[:size], to_both[size:]
    x_top = lax.ppermute(to_x[:half].astype(LOW), "seq", along)
    y_low = lax.ppermute(to_y[half:].astype(LOW), "seq", across)
    if early is not None:
        to_x, to_y = early(to_x, to_y)
    x_low = (to_x[half:] + via_y.astype(WIDE)).astype(LOW)
    y_top = (to_y[:half] + via_x.astype(WIDE)).astype(LOW)
    if sent is not None:
        sent(x_low, y_top)
    x_low = lax.ppermute(x_low, "seq", along)
    y_top = lax.ppermute(y_top, "seq", across)
    own = lax.optimization_barrier(partial(0, size))
    from_x = jnp.concatenate([x_top, x_low]).astype(WIDE)
    from_y = jnp.concatenate([y_top, y_low]).astype(WIDE)
    return own + from_x + from_y


def gather_width(shard):
    return lax.all_gather(shard, "dp", axis=0, tiled=True)


def line_pairs(first, last, step):
    return [(2 * i + c, 2 * (i + step) + c) for i in range(first, last + 1) for c in range(2)]


def core_pairs(planes):
    return swap_pairs(2 * planes, 1)


def row_block(rows):
    return next(size for size in (256, 128, 64, 32, 16) if rows % size == 0)


def column_block(columns):
    return next(size for size in (768, 512, 384, 256, 128) if columns % size == 0)


def this_core():
    return (lax.axis_index("dp") % 2).astype(jnp.int32).reshape(1)


def split_kernel(block, core, rows, parts):
    values = rows[...].astype(WIDE)
    pieces = [values[:, i : i + block] for i in range(0, values.shape[1], block)]
    even = jnp.concatenate(pieces[0::2], axis=1).astype(LOW)
    odd = jnp.concatenate(pieces[1::2], axis=1).astype(LOW)
    half = even.shape[1]

    @pl.when(core[0] == 0)
    def _():
        parts[:, :half] = even
        parts[:, half:] = odd

    @pl.when(core[0] != 0)
    def _():
        parts[:, :half] = odd
        parts[:, half:] = even


def by_core(rows):
    count, width = rows.shape
    size = row_block(count)
    whole = pl.BlockSpec((size, width), lambda i: (i, 0))
    return pl.pallas_call(
        functools.partial(split_kernel, width // lax.axis_size("dp")),
        out_shape=jax.ShapeDtypeStruct((count, width), LOW),
        grid=(count // size,),
        in_specs=[pl.BlockSpec(memory_space=pltpu.SMEM), whole],
        out_specs=whole,
        compiler_params=pltpu.CompilerParams(vmem_limit_bytes=VMEM_BYTES),
        name="split_columns",
    )(this_core(), rows)


def merge_kernel(early, late, out):
    count = lax.axis_size("dp")
    pieces = []
    for i in range(count):
        for part in (early, late):
            block = part.shape[1] // count
            pieces.append(part[:, i * block : (i + 1) * block])
    out[...] = jnp.concatenate(pieces, axis=1)


def merge_columns(early, late):
    count = early.shape[0]
    size = row_block(count)
    columns = early.shape[1] + late.shape[1]
    return pl.pallas_call(
        merge_kernel,
        out_shape=jax.ShapeDtypeStruct((count, columns), WIDE),
        grid=(count // size,),
        in_specs=[pl.BlockSpec((size, part.shape[1]), lambda i: (i, 0)) for part in (early, late)],
        out_specs=pl.BlockSpec((size, columns), lambda i: (i, 0)),
        compiler_params=pltpu.CompilerParams(vmem_limit_bytes=VMEM_BYTES),
        name="merge_columns",
    )(early, late)


def inner_kernel(planes, core, mine, other, w_early, w_late, gate, upward, to_gate, to_up):
    def part(rows, place):
        blocks = []
        for i in range(planes):
            for weight in (w_early, w_late):
                block = weight.shape[0] // planes // 2
                start = pl.multiple_of((2 * i + place) * block, block)
                blocks.append(weight[pl.ds(start, block), :])
        return jnp.dot(rows[...], jnp.concatenate(blocks), preferred_element_type=WIDE)

    grad = part(mine, core[0]) + part(other, 1 - core[0])
    value, slope = gelu_parts(gate[...].astype(WIDE))
    to_gate[...] = (grad * upward[...].astype(WIDE) * slope).astype(LOW)
    to_up[...] = (grad * value).astype(LOW)


def inner_back(mine, other, w_early, w_late, gate_up):
    count, half = other.shape
    units = gate_up.shape[1] // 2
    size = 256 if units % 256 == 0 else 128
    steps = units // size
    rows = pl.BlockSpec((count, half), lambda j: (0, 0))
    part = pl.BlockSpec((count, size), lambda j: (0, j))
    shape = jax.ShapeDtypeStruct((count, units), LOW)
    return pl.pallas_call(
        functools.partial(inner_kernel, lax.axis_size("dp") // 2),
        out_shape=[shape, shape],
        grid=(steps,),
        in_specs=[
            pl.BlockSpec(memory_space=pltpu.SMEM),
            rows,
            rows,
            pl.BlockSpec((w_early.shape[0], size), lambda j: (0, j)),
            pl.BlockSpec((w_late.shape[0], size), lambda j: (0, j)),
            part,
            pl.BlockSpec((count, size), lambda j: (0, j + steps)),
        ],
        out_specs=[part, part],
        compiler_params=pltpu.CompilerParams(vmem_limit_bytes=VMEM_BYTES),
        cost_estimate=pl.CostEstimate(flops=0, bytes_accessed=0, transcendentals=0),
        name="inner_back",
    )(this_core(), mine, other, w_early, w_late, gate_up, gate_up)


def first_kernel(left, right, more, out, turned):
    @pl.when(pl.program_id(0) == 0)
    def _():
        turned[...] = left[...].T

    total = jnp.dot(turned[...], right[...], preferred_element_type=WIDE)
    out[...] = (total + more[...].astype(WIDE)).astype(LOW)


def product_first(left, right, more):
    depth, rows = left.shape[0], left.shape[1] // 2
    columns = right.shape[1]
    size = column_block(columns)
    part = pl.BlockSpec((rows, size), lambda j: (0, j))
    return pl.pallas_call(
        first_kernel,
        out_shape=jax.ShapeDtypeStruct((rows, columns), LOW),
        grid=(columns // size,),
        in_specs=[
            pl.BlockSpec((depth, rows), lambda j: (0, 0)),
            pl.BlockSpec((depth, size), lambda j: (0, j)),
            part,
        ],
        out_specs=part,
        scratch_shapes=[pltpu.VMEM((rows, depth), LOW)],
        compiler_params=pltpu.CompilerParams(vmem_limit_bytes=VMEM_BYTES),
        cost_estimate=pl.CostEstimate(flops=0, bytes_accessed=0, transcendentals=0),
        name="product_first",
    )(left, right, more)


def product_kernel(left, right, *refs):
    total = jnp.dot(left[...], right[...], preferred_element_type=WIDE)
    if len(refs) == 2:
        total = total + refs[0][...].astype(WIDE)
    refs[-1][...] = total.astype(LOW)


def product(left, right, *more):
    rows, depth = left.shape
    columns = right.shape[1]
    size = column_block(columns)
    part = pl.BlockSpec((rows, size), lambda j: (0, j))
    return pl.pallas_call(
        product_kernel,
        out_shape=jax.ShapeDtypeStruct((rows, columns), LOW),
        grid=(columns // size,),
        in_specs=[
            pl.BlockSpec((rows, depth), lambda j: (0, 0)),
            pl.BlockSpec((depth, size), lambda j: (0, j)),
        ]
        + [part] * len(more),
        out_specs=part,
        compiler_params=pltpu.CompilerParams(vmem_limit_bytes=VMEM_BYTES),
        cost_estimate=pl.CostEstimate(flops=0, bytes_accessed=0, transcendentals=0),
        name="product",
    )(left, right, *more)


def attention_back_kernel(
    copies, q_scale, q, k, v, grad, probs, slopes, cosine, sine, out, grad_k, grad_v
):
    head, step = pl.program_id(0), pl.program_id(1)
    size, length = q.shape[0], k.shape[0]
    rows = pl.ds(pl.multiple_of(step * size, size), size)
    low = probs[0]
    grad_probs = dot_last(grad[...], v[...])
    across = jnp.sum(grad_probs * low.astype(WIDE), axis=-1, keepdims=True)
    grad_scores = (slopes[0].astype(WIDE) * (grad_probs - across)).astype(LOW)
    grad_q = rotate(dot(grad_scores, k[...]), cosine[rows, :], -sine[rows, :]) * q_scale
    out[rows, pl.ds(pl.multiple_of(head * HD, HD), HD)] = grad_q.astype(LOW)
    more_k = dot_first(grad_scores, q[...])
    more_v = dot_first(low, grad[...])
    first = (step == 0) & (head % copies == 0)

    @pl.when(first)
    def _():
        grad_k[...] = more_k
        grad_v[...] = more_v

    @pl.when(jnp.logical_not(first))
    def _():
        grad_k[...] += more_k
        grad_v[...] += more_v

    @pl.when((step == length // size - 1) & (head % copies == copies - 1))
    def _():
        heads = pl.num_programs(0)
        place = heads + head // copies
        to_k = pl.ds(pl.multiple_of(place * HD, HD), HD)
        to_v = pl.ds(pl.multiple_of((place + heads // copies) * HD, HD), HD)
        out[:, to_k] = rotate(grad_k[...], cosine[...], -sine[...]).astype(LOW)
        out[:, to_v] = grad_v[...].astype(LOW)


def attention_back(queries, keys, values, grad, probs, slopes, cosine, sine, q_scale):
    length, q_cols = queries.shape
    kv_cols = keys.shape[1]
    heads, copies = q_cols // HD, q_cols // kv_cols
    size = row_block(length)
    by_rows = pl.BlockSpec((size, HD), lambda h, i: (i, h))
    by_kv = pl.BlockSpec((length, HD), lambda h, i: (0, h // copies))
    scores = pl.BlockSpec((1, size, length), lambda h, i: (h, i, 0))
    angle = pl.BlockSpec((length, HD // 2), lambda h, i: (0, 0))
    columns = q_cols + 2 * kv_cols
    return pl.pallas_call(
        functools.partial(attention_back_kernel, copies, q_scale),
        out_shape=jax.ShapeDtypeStruct((length, columns), LOW),
        grid=(heads, length // size),
        in_specs=[by_rows, by_kv, by_kv, by_rows, scores, scores, angle, angle],
        out_specs=pl.BlockSpec((length, columns), lambda h, i: (0, 0)),
        scratch_shapes=[pltpu.VMEM((length, HD), WIDE)] * 2,
        compiler_params=pltpu.CompilerParams(vmem_limit_bytes=VMEM_BYTES),
        cost_estimate=pl.CostEstimate(flops=0, bytes_accessed=0, transcendentals=0),
        name="attention_back",
    )(queries, keys, values, grad, probs, slopes, cosine, sine)


def swap_cores(values):
    return lax.ppermute(values, "dp", core_pairs(lax.axis_size("dp") // 2))


def other_half(columns):
    return columns[:, columns.shape[1] // 2 :]


def give_core(columns, right):
    send = dot_first(other_half(columns), right).astype(LOW)
    send, columns = after(send, columns)
    return swap_cores(send), columns


def plane_sum(both):
    planes = lax.axis_size("dp") // 2
    groups = [[2 * i + c for i in range(planes)] for c in range(2)]
    return lax.psum_scatter(
        both, "dp", scatter_dimension=0, tiled=True, axis_index_groups=groups
    )


def after(value, *before):
    return lax.optimization_barrier((value,) + before)


class LineGather:
    def __init__(self, shard):
        self.planes = lax.axis_size("dp") // 2
        self.shard = self.risen = self.sunk = shard
        self.below, self.above = [], []

    def advance(self, *before):
        step, last = len(self.below), self.planes - 1
        if step == last:
            return
        risen, sunk = after(self.risen, self.sunk, *before)[:2]
        self.risen = lax.ppermute(risen, "dp", line_pairs(step, last - 1, 1))
        self.sunk = lax.ppermute(sunk, "dp", line_pairs(1, last - step, -1))
        self.below.insert(0, self.risen)
        self.above.append(self.sunk)

    def whole(self):
        for _ in range(self.planes - 1):
            self.advance()
        place = lax.axis_index("dp")
        plane, core = place // 2, place % 2
        held = jnp.stack(self.below + [self.shard] + self.above)
        held = lax.dynamic_slice_in_dim(held, self.planes - 1 - plane, self.planes, 0)
        other = swap_cores(held)
        even = jnp.where(core == 0, held, other)
        odd = jnp.where(core == 0, other, held)
        rows = 2 * self.planes * self.shard.shape[0]
        return jnp.stack([even, odd], axis=1).reshape(rows, self.shard.shape[1])


def dot(left, right):
    return jnp.dot(left, right, preferred_element_type=WIDE)


def dot_last(left, right):
    return lax.dot_general(left, right, (((1,), (1,)), ((), ())), preferred_element_type=WIDE)


def dot_first(left, right):
    return lax.dot_general(left, right, (((0,), (0,)), ((), ())), preferred_element_type=WIDE)


def norm_factor(values):
    return lax.rsqrt(jnp.mean(values * values, axis=-1, keepdims=True) + EPSILON)


def norm_back(values, factor, scale, grad):
    scaled = grad * scale
    inner = jnp.mean(scaled * values, axis=-1, keepdims=True)
    back = factor * scaled - values * (factor * factor * factor * inner)
    return back, jnp.sum(grad * values * factor, axis=0)


def rotate(values, cosine, sine):
    half = values.shape[1] // 2
    left = values[:, :half]
    right = values[:, half:]
    return jnp.concatenate([left * cosine - right * sine, right * cosine + left * sine], axis=1)


def gelu_parts(gate):
    scale = 0.7978845608028654
    square_gate = gate * gate
    turn = jnp.tanh(scale * (gate + 0.044715 * (square_gate * gate)))
    value = 0.5 * gate * (1.0 + turn)
    slope = 0.5 * (1.0 + turn) + 0.5 * gate * (1.0 - turn * turn) * (
        scale * (1.0 + 3.0 * 0.044715 * square_gate)
    )
    return value, slope


def shards(
    tokens,
    query_weight,
    key_weight,
    value_weight,
    output_weight,
    attn_norm,
    post_attn_norm,
    ffn_norm,
    post_ffn_norm,
    gate_weight,
    up_weight,
    down_weight,
    cotangent,
):
    size, width = tokens.shape
    seq_count = lax.axis_size("seq")
    dp_count = lax.axis_size("dp")
    heads = HQ // seq_count
    sharing = max(1, seq_count // HK)
    groups = [[first + i for i in range(sharing)] for first in range(0, seq_count, sharing)]
    kv_heads = max(1, HK // seq_count)
    copies = heads // kv_heads

    if sharing > 1:
        key_weight = lax.all_gather(
            key_weight, "seq", axis=1, tiled=True, axis_index_groups=groups
        )
        value_weight = lax.all_gather(
            value_weight, "seq", axis=1, tiled=True, axis_index_groups=groups
        )
    q_cols, kv_cols = heads * HD, kv_heads * HD
    hidden_units = gate_weight.shape[1]
    first_value = q_cols + kv_cols
    all_cols = first_value + kv_cols
    w_attn = gather_width(
        jnp.concatenate([query_weight, key_weight, value_weight, output_weight], axis=1)
    )
    w_ffn = gather_width(jnp.concatenate([gate_weight, up_weight], axis=1))
    early = down_weight.shape[0] * 5 // 9 // 16 * 16
    w_late = gather_width(down_weight[early:])
    w_qkv, w_output = w_attn[:, :all_cols], w_attn[:, all_cols:]

    stacked = jnp.stack([attn_norm, post_attn_norm, ffn_norm, post_ffn_norm])
    scales = gather_small(stacked, "dp").transpose(1, 0, 2).reshape(4, width)
    early_shard, scales = after(down_weight[:early], scales)
    line = LineGather(early_shard)
    line.advance()
    line.advance()
    scales = 1.0 + scales.astype(WIDE)
    scale_one, scale_two, scale_three, scale_four = (scales[i : i + 1] for i in range(4))

    whole_tokens = gather_rows(tokens).astype(WIDE)
    normed = (whole_tokens * norm_factor(whole_tokens) * scale_one).astype(LOW)
    normed_cols = by_core(normed)
    length = size * seq_count
    places = (chunk_places(seq_count)[:, None] * size + jnp.arange(size)[None, :]).reshape(length)
    half = HD // 2
    freqs = 10000.0 ** (-jnp.arange(half).astype(WIDE) / half)
    angles = places.astype(WIDE)[:, None] * freqs[None, :]
    cosine, sine = jnp.cos(angles), jnp.sin(angles)
    allowed = (places[None, :] <= places[:, None]) & (
        places[:, None] - places[None, :] < WINDOW
    )
    q_scale = HD ** (-0.5)
    linear = dot(normed, w_qkv)
    parts = [linear[:, i * HD : (i + 1) * HD] for i in range(heads + 2 * kv_heads)]
    queries = [(rotate(part, cosine, sine) * q_scale).astype(LOW) for part in parts[:heads]]
    keys = [rotate(part, cosine, sine).astype(LOW) for part in parts[heads : heads + kv_heads]]
    values = [part.astype(LOW) for part in parts[heads + kv_heads :]]
    probs, slopes, head_outs = [], [], []
    for h in range(heads):
        turn = jnp.tanh(dot_last(queries[h], keys[h // copies]) / SOFT_CAP)
        capped = jnp.where(allowed, SOFT_CAP * turn, -1e30)
        highest = jnp.max(capped, axis=-1, keepdims=True)
        weights = jnp.exp(capped - highest)
        prob = weights / jnp.sum(weights, axis=-1, keepdims=True)
        probs.append(prob.astype(LOW))
        slopes.append((prob * (1.0 - turn * turn)).astype(LOW))
        head_outs.append(dot(probs[h], values[h // copies]).astype(LOW))
    probs, slopes = jnp.stack(probs), jnp.stack(slopes)
    queries, keys, values = (jnp.concatenate(item, axis=1) for item in (queries, keys, values))
    mixed = jnp.concatenate(head_outs, axis=1)
    mixed, queries, keys, values, probs, slopes = after(
        mixed, queries, keys, values, probs, slopes
    )
    line.advance(mixed)
    w_early = line.whole()
    projected = scatter_rows(lambda a, b: dot_last(mixed[a:b], w_output), size)

    inputs = tokens.astype(WIDE)
    factor_two = norm_factor(projected)
    hidden = inputs + projected * factor_two * scale_two
    factor_three = norm_factor(hidden)
    whole_in = gather_rows((hidden * factor_three * scale_three).astype(LOW))
    gate_up = lax.optimization_barrier(dot(whole_in, w_ffn).astype(LOW))
    gate, upward = gate_up[:, :hidden_units].astype(WIDE), gate_up[:, hidden_units:].astype(WIDE)
    inner = lax.optimization_barrier((gelu_parts(gate)[0] * upward).astype(LOW))
    in_cols = by_core(whole_in)
    in_mine, in_other = in_cols[:, : width // 2].T, other_half(in_cols).T
    in_mine, in_other, inner = after(in_mine, in_other, inner)
    given = swap_cores(inner)

    def early_sent(*rows):
        nonlocal w_late
        w_late = after(w_late, *rows)[0]

    early_raw = scatter_rows(
        lambda a, b: dot_last(inner[a:b], w_early), size, sent=early_sent
    )
    late_raw = scatter_rows(lambda a, b: dot_last(inner[a:b], w_late), size)
    ffn_raw = merge_columns(early_raw, late_raw)
    factor_four = norm_factor(ffn_raw)
    result = (hidden + ffn_raw * factor_four * scale_four).astype(LOW)

    grad_result = cotangent.astype(WIDE)
    grad_raw, grad_scale_four = norm_back(ffn_raw, factor_four, scale_four, grad_result)
    grad_cols = by_core(grad_raw.astype(LOW))
    half = width // 2
    both_grad = gather_rows(
        jnp.concatenate([grad_cols[:, :half], swap_cores(other_half(grad_cols))]), halves=True
    )
    both_grad = lax.optimization_barrier(both_grad)
    own_down = lax.optimization_barrier(dot_first(both_grad[:length], inner).astype(LOW))
    sum_down = dot_first(both_grad[length:], given) + own_down.astype(WIDE)
    sum_down = sum_down.astype(LOW)
    sum_down, both_grad = after(sum_down, both_grad)
    grad_other = swap_cores(both_grad[length:])
    down_low = plane_sum(sum_down)
    grad_gate, grad_up = inner_back(both_grad, grad_other, w_early, w_late, gate_up)
    send, grad_gate, grad_up = after(product(in_other, grad_gate), grad_gate, grad_up)
    got_gate = swap_cores(send)
    gate_low = None

    def ffn_in_early(*rows):
        nonlocal grad_gate, grad_up, down_low, gate_low
        held = after(grad_gate, *rows)
        sum_gate = product(in_mine, held[0], got_gate)
        held = after(sum_gate, *held[1:])
        sum_gate, grad_gate, grad_up, down_low = after(held[0], grad_gate, grad_up, down_low)
        gate_low = plane_sum(sum_gate)
        return held[1:]

    def ffn_in_rows(start, stop):
        return dot_last(grad_gate[start:stop], w_ffn[:, :hidden_units]) + dot_last(
            grad_up[start:stop], w_ffn[:, hidden_units:]
        )

    grad_ffn_in = scatter_rows(ffn_in_rows, size, ffn_in_early)
    send, grad_up = after(product(in_other, grad_up), grad_up)
    sum_up = product(in_mine, grad_up, swap_cores(send))
    back_three, grad_scale_three = norm_back(hidden, factor_three, scale_three, grad_ffn_in)
    grad_hidden = grad_result + back_three
    back_two, grad_scale_two = norm_back(projected, factor_two, scale_two, grad_hidden)
    up_low = None

    def proj_between(*rows):
        nonlocal up_low
        held = after(sum_up, *rows)
        up_low = plane_sum(held[0])
        return held[1:]

    whole_proj = gather_rows(back_two.astype(LOW), proj_between)
    got, proj_cols = give_core(by_core(whole_proj), mixed)
    sum_output = product_first(proj_cols, mixed, got)
    sum_output, whole_proj = after(sum_output, whole_proj)
    grad_mixed = dot(whole_proj, w_output).astype(LOW)

    grad_linear = attention_back(
        queries, keys, values, grad_mixed, probs, slopes, cosine, sine, q_scale
    )
    got, normed_cols = give_core(normed_cols, grad_linear)
    attn_low = None

    def normed_sent(*rows):
        nonlocal attn_low, gate_low, up_low
        sum_attn = product_first(normed_cols, grad_linear, got)
        sum_attn = jnp.concatenate([sum_attn, sum_output], axis=1)
        sum_attn = after(sum_attn, *rows)[0]
        sum_attn, gate_low, up_low = after(sum_attn, gate_low, up_low)
        attn_low = plane_sum(sum_attn)

    grad_normed = scatter_rows(lambda a, b: dot_last(grad_linear[a:b], w_qkv), size, sent=normed_sent)
    back_one, grad_scale_one = norm_back(inputs, norm_factor(inputs), scale_one, grad_normed)
    grad_tokens = grad_hidden + back_one

    shard_down, shard_gate, shard_up, shard_attn = (
        item.astype(WIDE) for item in (down_low, gate_low, up_low, attn_low)
    )
    shard_query = shard_attn[:, :q_cols]
    shard_output = shard_attn[:, all_cols:]
    shard_key = shard_attn[:, q_cols:first_value]
    shard_value = shard_attn[:, first_value:all_cols]
    if sharing > 1:
        shard_key, shard_value = (
            lax.psum_scatter(
                item.astype(LOW),
                "seq",
                scatter_dimension=1,
                tiled=True,
                axis_index_groups=groups,
            ).astype(WIDE)
            for item in (shard_key, shard_value)
        )

    piece = width // (dp_count * seq_count)
    stacked = jnp.stack([grad_scale_one, grad_scale_two, grad_scale_three, grad_scale_four])
    packed = stacked.reshape(4, dp_count, seq_count, piece).transpose(1, 2, 0, 3)
    packed = packed.reshape(dp_count, seq_count, 4 * piece)
    owned = scatter_small(scatter_small(packed, "dp"), "seq").reshape(4, piece)
    return (
        result,
        grad_tokens,
        shard_query,
        shard_key,
        shard_value,
        shard_output,
        owned[0],
        owned[1],
        owned[2],
        owned[3],
        shard_gate,
        shard_up,
        shard_down,
    )


def solution(mesh):
    rows = P(("dp", "seq"), None)
    weight = P("dp", "seq")
    scale = P("dp")
    scale_grad = P(("dp", "seq"))
    in_specs = (
        (rows,) + (weight,) * 4 + (scale,) * 4 + (weight,) * 3 + (rows,)
    )
    out_specs = (rows, rows) + (weight,) * 4 + (scale_grad,) * 4 + (weight,) * 3
    return jax.shard_map(
        shards, mesh=mesh, in_specs=in_specs, out_specs=out_specs, check_vma=False
    )
```

```python
import functools

import jax
import jax.numpy as jnp
from jax import lax
from jax.experimental import pallas as pl
from jax.experimental.pallas import tpu as pltpu
from jax.sharding import PartitionSpec as P

HQ = 8
HK = 4
HD = 256
WINDOW = 4096
EPSILON = 1e-06
SOFT_CAP = 50.0
LOW = jnp.bfloat16
WIDE = jnp.float32
VMEM_BYTES = 48 * 1024 * 1024


def swap_pairs(count, mask):
    return [(i, i ^ mask) for i in range(count)]


def gather_small(values, axis):
    count = lax.axis_size(axis)
    if count & (count - 1):
        return lax.all_gather(values, axis, axis=0, tiled=False)
    place = lax.axis_index(axis)
    held = values[None]
    bit = 1
    while bit < count:
        other = lax.ppermute(held, axis, swap_pairs(count, bit))
        upper = (place & bit) != 0
        held = jnp.where(
            upper, jnp.concatenate([other, held]), jnp.concatenate([held, other])
        )
        bit *= 2
    return held


def scatter_small(values, axis):
    count = lax.axis_size(axis)
    if count & (count - 1):
        return lax.psum_scatter(values, axis, scatter_dimension=0, tiled=False)
    place = lax.axis_index(axis)
    bit = count // 2
    while bit:
        halves = values.reshape((2, bit) + values.shape[1:])
        upper = (place & bit) != 0
        keep = jnp.where(upper, halves[1], halves[0])
        send = jnp.where(upper, halves[0], halves[1])
        values = keep + lax.ppermute(send, axis, swap_pairs(count, bit))
        bit //= 2
    return values[0]


def square(count):
    return count == 4


def chunk_places(count):
    here = lax.axis_index("seq")
    if square(count):
        return here ^ jnp.arange(count)
    return jnp.arange(count)


def gather_rows(rows, between=None, halves=False):
    count = lax.axis_size("seq")
    if not square(count):
        if between is not None:
            (rows,) = between(rows)
        rows = lax.all_gather(rows, "seq", axis=0, tiled=not halves)
        if halves:
            rows = rows.reshape(count, 2, -1, rows.shape[2]).transpose(1, 0, 2, 3)
            rows = rows.reshape(-1, rows.shape[3])
        return rows
    half = rows.shape[0] // 2
    along, across = swap_pairs(count, 1), swap_pairs(count, 2)
    top, low = rows[:half], rows[half:]
    y_top = lax.ppermute(top, "seq", across)
    x_low = lax.ppermute(low, "seq", along)
    y_low = lax.ppermute(low, "seq", across)
    x_top = lax.ppermute(top, "seq", along)
    if between is not None:
        y_top, x_low = between(y_top, x_low)
    far_top = lax.ppermute(y_top, "seq", along)
    far_low = lax.ppermute(x_low, "seq", across)
    if halves:
        return jnp.concatenate([top, x_top, y_top, far_top, low, x_low, y_low, far_low])
    return jnp.concatenate([rows, x_top, x_low, y_top, y_low, far_top, far_low])


def scatter_rows(partial, size, early=None, sent=None):
    count = lax.axis_size("seq")
    if not square(count):
        rows = partial(0, count * size).astype(LOW)
        if early is not None:
            (rows,) = early(rows)
        if sent is not None:
            sent(rows)
        return lax.psum_scatter(rows, "seq", scatter_dimension=0, tiled=True).astype(WIDE)
    half = size // 2
    along, across = swap_pairs(count, 1), swap_pairs(count, 2)
    far = partial(3 * size, 4 * size).astype(LOW)
    via_x = lax.ppermute(far[:half], "seq", along)
    via_y = lax.ppermute(far[half:], "seq", across)
    to_both = partial(size, 3 * size)
    to_x, to_y = to_both[:size], to_both[size:]
    x_top = lax.ppermute(to_x[:half].astype(LOW), "seq", along)
    y_low = lax.ppermute(to_y[half:].astype(LOW), "seq", across)
    if early is not None:
        to_x, to_y = early(to_x, to_y)
    x_low = (to_x[half:] + via_y.astype(WIDE)).astype(LOW)
    y_top = (to_y[:half] + via_x.astype(WIDE)).astype(LOW)
    if sent is not None:
        sent(x_low, y_top)
    x_low = lax.ppermute(x_low, "seq", along)
    y_top = lax.ppermute(y_top, "seq", across)
    own = lax.optimization_barrier(partial(0, size))
    from_x = jnp.concatenate([x_top, x_low]).astype(WIDE)
    from_y = jnp.concatenate([y_top, y_low]).astype(WIDE)
    return own + from_x + from_y


def gather_width(shard):
    return lax.all_gather(shard, "dp", axis=0, tiled=True)


def line_pairs(first, last, step):
    return [(2 * i + c, 2 * (i + step) + c) for i in range(first, last + 1) for c in range(2)]


def core_pairs(planes):
    return swap_pairs(2 * planes, 1)


def row_block(rows):
    return next(size for size in (256, 128, 64, 32, 16) if rows % size == 0)


def column_block(columns):
    return next(size for size in (768, 512, 384, 256, 128) if columns % size == 0)


def this_core():
    return (lax.axis_index("dp") % 2).astype(jnp.int32).reshape(1)


def split_kernel(block, core, rows, parts):
    values = rows[...].astype(WIDE)
    pieces = [values[:, i : i + block] for i in range(0, values.shape[1], block)]
    even = jnp.concatenate(pieces[0::2], axis=1).astype(LOW)
    odd = jnp.concatenate(pieces[1::2], axis=1).astype(LOW)
    half = even.shape[1]

    @pl.when(core[0] == 0)
    def _():
        parts[:, :half] = even
        parts[:, half:] = odd

    @pl.when(core[0] != 0)
    def _():
        parts[:, :half] = odd
        parts[:, half:] = even


def by_core(rows):
    count, width = rows.shape
    size = row_block(count)
    whole = pl.BlockSpec((size, width), lambda i: (i, 0))
    return pl.pallas_call(
        functools.partial(split_kernel, width // lax.axis_size("dp")),
        out_shape=jax.ShapeDtypeStruct((count, width), LOW),
        grid=(count // size,),
        in_specs=[pl.BlockSpec(memory_space=pltpu.SMEM), whole],
        out_specs=whole,
        compiler_params=pltpu.CompilerParams(vmem_limit_bytes=VMEM_BYTES),
        name="split_columns",
    )(this_core(), rows)


def merge_kernel(early, late, out):
    count = lax.axis_size("dp")
    pieces = []
    for i in range(count):
        for part in (early, late):
            block = part.shape[1] // count
            pieces.append(part[:, i * block : (i + 1) * block])
    out[...] = jnp.concatenate(pieces, axis=1)


def merge_columns(early, late):
    count = early.shape[0]
    size = row_block(count)
    columns = early.shape[1] + late.shape[1]
    return pl.pallas_call(
        merge_kernel,
        out_shape=jax.ShapeDtypeStruct((count, columns), WIDE),
        grid=(count // size,),
        in_specs=[pl.BlockSpec((size, part.shape[1]), lambda i: (i, 0)) for part in (early, late)],
        out_specs=pl.BlockSpec((size, columns), lambda i: (i, 0)),
        compiler_params=pltpu.CompilerParams(vmem_limit_bytes=VMEM_BYTES),
        name="merge_columns",
    )(early, late)


def inner_kernel(planes, core, mine, other, w_early, w_late, gate, upward, to_gate, to_up):
    def part(rows, place):
        blocks = []
        for i in range(planes):
            for weight in (w_early, w_late):
                block = weight.shape[0] // planes // 2
                start = pl.multiple_of((2 * i + place) * block, block)
                blocks.append(weight[pl.ds(start, block), :])
        return jnp.dot(rows[...], jnp.concatenate(blocks), preferred_element_type=WIDE)

    grad = part(mine, core[0]) + part(other, 1 - core[0])
    value, slope = gelu_parts(gate[...].astype(WIDE))
    to_gate[...] = (grad * upward[...].astype(WIDE) * slope).astype(LOW)
    to_up[...] = (grad * value).astype(LOW)


def inner_back(mine, other, w_early, w_late, gate_up):
    count, half = other.shape
    units = gate_up.shape[1] // 2
    size = 256 if units % 256 == 0 else 128
    steps = units // size
    rows = pl.BlockSpec((count, half), lambda j: (0, 0))
    part = pl.BlockSpec((count, size), lambda j: (0, j))
    shape = jax.ShapeDtypeStruct((count, units), LOW)
    return pl.pallas_call(
        functools.partial(inner_kernel, lax.axis_size("dp") // 2),
        out_shape=[shape, shape],
        grid=(steps,),
        in_specs=[
            pl.BlockSpec(memory_space=pltpu.SMEM),
            rows,
            rows,
            pl.BlockSpec((w_early.shape[0], size), lambda j: (0, j)),
            pl.BlockSpec((w_late.shape[0], size), lambda j: (0, j)),
            part,
            pl.BlockSpec((count, size), lambda j: (0, j + steps)),
        ],
        out_specs=[part, part],
        compiler_params=pltpu.CompilerParams(vmem_limit_bytes=VMEM_BYTES),
        cost_estimate=pl.CostEstimate(flops=0, bytes_accessed=0, transcendentals=0),
        name="inner_back",
    )(this_core(), mine, other, w_early, w_late, gate_up, gate_up)


def first_kernel(left, right, more, out, turned):
    @pl.when(pl.program_id(0) == 0)
    def _():
        turned[...] = left[...].T

    total = jnp.dot(turned[...], right[...], preferred_element_type=WIDE)
    out[...] = (total + more[...].astype(WIDE)).astype(LOW)


def product_first(left, right, more):
    depth, rows = left.shape[0], left.shape[1] // 2
    columns = right.shape[1]
    size = column_block(columns)
    part = pl.BlockSpec((rows, size), lambda j: (0, j))
    return pl.pallas_call(
        first_kernel,
        out_shape=jax.ShapeDtypeStruct((rows, columns), LOW),
        grid=(columns // size,),
        in_specs=[
            pl.BlockSpec((depth, rows), lambda j: (0, 0)),
            pl.BlockSpec((depth, size), lambda j: (0, j)),
            part,
        ],
        out_specs=part,
        scratch_shapes=[pltpu.VMEM((rows, depth), LOW)],
        compiler_params=pltpu.CompilerParams(vmem_limit_bytes=VMEM_BYTES),
        cost_estimate=pl.CostEstimate(flops=0, bytes_accessed=0, transcendentals=0),
        name="product_first",
    )(left, right, more)


def product_kernel(left, right, *refs):
    total = jnp.dot(left[...], right[...], preferred_element_type=WIDE)
    if len(refs) == 2:
        total = total + refs[0][...].astype(WIDE)
    refs[-1][...] = total.astype(LOW)


def product(left, right, *more):
    rows, depth = left.shape
    columns = right.shape[1]
    size = column_block(columns)
    part = pl.BlockSpec((rows, size), lambda j: (0, j))
    return pl.pallas_call(
        product_kernel,
        out_shape=jax.ShapeDtypeStruct((rows, columns), LOW),
        grid=(columns // size,),
        in_specs=[
            pl.BlockSpec((rows, depth), lambda j: (0, 0)),
            pl.BlockSpec((depth, size), lambda j: (0, j)),
        ]
        + [part] * len(more),
        out_specs=part,
        compiler_params=pltpu.CompilerParams(vmem_limit_bytes=VMEM_BYTES),
        cost_estimate=pl.CostEstimate(flops=0, bytes_accessed=0, transcendentals=0),
        name="product",
    )(left, right, *more)


def attention_back_kernel(
    copies, q_scale, q, k, v, grad, probs, slopes, cosine, sine, out, grad_k, grad_v
):
    head, step = pl.program_id(0), pl.program_id(1)
    size, length = q.shape[0], k.shape[0]
    rows = pl.ds(pl.multiple_of(step * size, size), size)
    low = probs[0]
    grad_probs = dot_last(grad[...], v[...])
    across = jnp.sum(grad_probs * low.astype(WIDE), axis=-1, keepdims=True)
    grad_scores = (slopes[0].astype(WIDE) * (grad_probs - across)).astype(LOW)
    grad_q = rotate(dot(grad_scores, k[...]), cosine[rows, :], -sine[rows, :]) * q_scale
    out[rows, pl.ds(pl.multiple_of(head * HD, HD), HD)] = grad_q.astype(LOW)
    more_k = dot_first(grad_scores, q[...])
    more_v = dot_first(low, grad[...])
    first = (step == 0) & (head % copies == 0)

    @pl.when(first)
    def _():
        grad_k[...] = more_k
        grad_v[...] = more_v

    @pl.when(jnp.logical_not(first))
    def _():
        grad_k[...] += more_k
        grad_v[...] += more_v

    @pl.when((step == length // size - 1) & (head % copies == copies - 1))
    def _():
        heads = pl.num_programs(0)
        place = heads + head // copies
        to_k = pl.ds(pl.multiple_of(place * HD, HD), HD)
        to_v = pl.ds(pl.multiple_of((place + heads // copies) * HD, HD), HD)
        out[:, to_k] = rotate(grad_k[...], cosine[...], -sine[...]).astype(LOW)
        out[:, to_v] = grad_v[...].astype(LOW)


def attention_back(queries, keys, values, grad, probs, slopes, cosine, sine, q_scale):
    length, q_cols = queries.shape
    kv_cols = keys.shape[1]
    heads, copies = q_cols // HD, q_cols // kv_cols
    size = row_block(length)
    by_rows = pl.BlockSpec((size, HD), lambda h, i: (i, h))
    by_kv = pl.BlockSpec((length, HD), lambda h, i: (0, h // copies))
    scores = pl.BlockSpec((1, size, length), lambda h, i: (h, i, 0))
    angle = pl.BlockSpec((length, HD // 2), lambda h, i: (0, 0))
    columns = q_cols + 2 * kv_cols
    return pl.pallas_call(
        functools.partial(attention_back_kernel, copies, q_scale),
        out_shape=jax.ShapeDtypeStruct((length, columns), LOW),
        grid=(heads, length // size),
        in_specs=[by_rows, by_kv, by_kv, by_rows, scores, scores, angle, angle],
        out_specs=pl.BlockSpec((length, columns), lambda h, i: (0, 0)),
        scratch_shapes=[pltpu.VMEM((length, HD), WIDE)] * 2,
        compiler_params=pltpu.CompilerParams(vmem_limit_bytes=VMEM_BYTES),
        cost_estimate=pl.CostEstimate(flops=0, bytes_accessed=0, transcendentals=0),
        name="attention_back",
    )(queries, keys, values, grad, probs, slopes, cosine, sine)


def swap_cores(values):
    return lax.ppermute(values, "dp", core_pairs(lax.axis_size("dp") // 2))


def other_half(columns):
    return columns[:, columns.shape[1] // 2 :]


def give_core(columns, right):
    send = dot_first(other_half(columns), right).astype(LOW)
    send, columns = after(send, columns)
    return swap_cores(send), columns


def plane_sum(both):
    planes = lax.axis_size("dp") // 2
    groups = [[2 * i + c for i in range(planes)] for c in range(2)]
    return lax.psum_scatter(
        both, "dp", scatter_dimension=0, tiled=True, axis_index_groups=groups
    )


def after(value, *before):
    return lax.optimization_barrier((value,) + before)


class LineGather:
    def __init__(self, shard):
        self.planes = lax.axis_size("dp") // 2
        self.shard = self.risen = self.sunk = shard
        self.below, self.above = [], []

    def advance(self, *before):
        step, last = len(self.below), self.planes - 1
        if step == last:
            return
        risen, sunk = after(self.risen, self.sunk, *before)[:2]
        self.risen = lax.ppermute(risen, "dp", line_pairs(step, last - 1, 1))
        self.sunk = lax.ppermute(sunk, "dp", line_pairs(1, last - step, -1))
        self.below.insert(0, self.risen)
        self.above.append(self.sunk)

    def whole(self):
        for _ in range(self.planes - 1):
            self.advance()
        place = lax.axis_index("dp")
        plane, core = place // 2, place % 2
        held = jnp.stack(self.below + [self.shard] + self.above)
        held = lax.dynamic_slice_in_dim(held, self.planes - 1 - plane, self.planes, 0)
        other = swap_cores(held)
        even = jnp.where(core == 0, held, other)
        odd = jnp.where(core == 0, other, held)
        rows = 2 * self.planes * self.shard.shape[0]
        return jnp.stack([even, odd], axis=1).reshape(rows, self.shard.shape[1])


def dot(left, right):
    return jnp.dot(left, right, preferred_element_type=WIDE)


def dot_last(left, right):
    return lax.dot_general(left, right, (((1,), (1,)), ((), ())), preferred_element_type=WIDE)


def dot_first(left, right):
    return lax.dot_general(left, right, (((0,), (0,)), ((), ())), preferred_element_type=WIDE)


def norm_factor(values):
    return lax.rsqrt(jnp.mean(values * values, axis=-1, keepdims=True) + EPSILON)


def norm_back(values, factor, scale, grad):
    scaled = grad * scale
    inner = jnp.mean(scaled * values, axis=-1, keepdims=True)
    back = factor * scaled - values * (factor * factor * factor * inner)
    return back, jnp.sum(grad * values * factor, axis=0)


def rotate(values, cosine, sine):
    half = values.shape[1] // 2
    left = values[:, :half]
    right = values[:, half:]
    return jnp.concatenate([left * cosine - right * sine, right * cosine + left * sine], axis=1)


def gelu_parts(gate):
    scale = 0.7978845608028654
    square_gate = gate * gate
    turn = jnp.tanh(scale * (gate + 0.044715 * (square_gate * gate)))
    value = 0.5 * gate * (1.0 + turn)
    slope = 0.5 * (1.0 + turn) + 0.5 * gate * (1.0 - turn * turn) * (
        scale * (1.0 + 3.0 * 0.044715 * square_gate)
    )
    return value, slope


def shards(
    tokens,
    query_weight,
    key_weight,
    value_weight,
    output_weight,
    attn_norm,
    post_attn_norm,
    ffn_norm,
    post_ffn_norm,
    gate_weight,
    up_weight,
    down_weight,
    cotangent,
):
    size, width = tokens.shape
    seq_count = lax.axis_size("seq")
    dp_count = lax.axis_size("dp")
    heads = HQ // seq_count
    sharing = max(1, seq_count // HK)
    groups = [[first + i for i in range(sharing)] for first in range(0, seq_count, sharing)]
    kv_heads = max(1, HK // seq_count)
    copies = heads // kv_heads

    if sharing > 1:
        key_weight = lax.all_gather(
            key_weight, "seq", axis=1, tiled=True, axis_index_groups=groups
        )
        value_weight = lax.all_gather(
            value_weight, "seq", axis=1, tiled=True, axis_index_groups=groups
        )
    q_cols, kv_cols = heads * HD, kv_heads * HD
    hidden_units = gate_weight.shape[1]
    first_value = q_cols + kv_cols
    all_cols = first_value + kv_cols
    w_attn = gather_width(
        jnp.concatenate([query_weight, key_weight, value_weight, output_weight], axis=1)
    )
    w_ffn = gather_width(jnp.concatenate([gate_weight, up_weight], axis=1))
    early = down_weight.shape[0] * 5 // 9 // 16 * 16
    w_late = gather_width(down_weight[early:])
    w_qkv, w_output = w_attn[:, :all_cols], w_attn[:, all_cols:]

    stacked = jnp.stack([attn_norm, post_attn_norm, ffn_norm, post_ffn_norm])
    scales = gather_small(stacked, "dp").transpose(1, 0, 2).reshape(4, width)
    early_shard, scales = after(down_weight[:early], scales)
    line = LineGather(early_shard)
    line.advance()
    line.advance()
    scales = 1.0 + scales.astype(WIDE)
    scale_one, scale_two, scale_three, scale_four = (scales[i : i + 1] for i in range(4))

    whole_tokens = gather_rows(tokens).astype(WIDE)
    normed = (whole_tokens * norm_factor(whole_tokens) * scale_one).astype(LOW)
    normed_cols = by_core(normed)
    length = size * seq_count
    places = (chunk_places(seq_count)[:, None] * size + jnp.arange(size)[None, :]).reshape(length)
    half = HD // 2
    freqs = 10000.0 ** (-jnp.arange(half).astype(WIDE) / half)
    angles = places.astype(WIDE)[:, None] * freqs[None, :]
    cosine, sine = jnp.cos(angles), jnp.sin(angles)
    allowed = (places[None, :] <= places[:, None]) & (
        places[:, None] - places[None, :] < WINDOW
    )
    q_scale = HD ** (-0.5)
    linear = dot(normed, w_qkv)
    parts = [linear[:, i * HD : (i + 1) * HD] for i in range(heads + 2 * kv_heads)]
    queries = [(rotate(part, cosine, sine) * q_scale).astype(LOW) for part in parts[:heads]]
    keys = [rotate(part, cosine, sine).astype(LOW) for part in parts[heads : heads + kv_heads]]
    values = [part.astype(LOW) for part in parts[heads + kv_heads :]]
    probs, slopes, head_outs = [], [], []
    for h in range(heads):
        turn = jnp.tanh(dot_last(queries[h], keys[h // copies]) / SOFT_CAP)
        capped = jnp.where(allowed, SOFT_CAP * turn, -1e30)
        highest = jnp.max(capped, axis=-1, keepdims=True)
        weights = jnp.exp(capped - highest)
        prob = weights / jnp.sum(weights, axis=-1, keepdims=True)
        probs.append(prob.astype(LOW))
        slopes.append((prob * (1.0 - turn * turn)).astype(LOW))
        head_outs.append(dot(probs[h], values[h // copies]).astype(LOW))
    probs, slopes = jnp.stack(probs), jnp.stack(slopes)
    queries, keys, values = (jnp.concatenate(item, axis=1) for item in (queries, keys, values))
    mixed = jnp.concatenate(head_outs, axis=1)
    mixed, queries, keys, values, probs, slopes = after(
        mixed, queries, keys, values, probs, slopes
    )
    line.advance(mixed)
    w_early = line.whole()
    projected = scatter_rows(lambda a, b: dot_last(mixed[a:b], w_output), size)

    inputs = tokens.astype(WIDE)
    factor_two = norm_factor(projected)
    hidden = inputs + projected * factor_two * scale_two
    factor_three = norm_factor(hidden)
    whole_in = gather_rows((hidden * factor_three * scale_three).astype(LOW))
    gate_up = lax.optimization_barrier(dot(whole_in, w_ffn).astype(LOW))
    gate, upward = gate_up[:, :hidden_units].astype(WIDE), gate_up[:, hidden_units:].astype(WIDE)
    inner = lax.optimization_barrier((gelu_parts(gate)[0] * upward).astype(LOW))
    in_cols = by_core(whole_in)
    in_mine, in_other = in_cols[:, : width // 2].T, other_half(in_cols).T
    in_mine, in_other, inner = after(in_mine, in_other, inner)
    given = swap_cores(inner)

    def early_sent(*rows):
        nonlocal w_late
        w_late = after(w_late, *rows)[0]

    early_raw = scatter_rows(
        lambda a, b: dot_last(inner[a:b], w_early), size, sent=early_sent
    )

    def late_early(*rows):
        nonlocal early_raw
        early_raw, *rows = after(early_raw, *rows)
        return rows

    late_raw = scatter_rows(lambda a, b: dot_last(inner[a:b], w_late), size, late_early)
    ffn_raw = merge_columns(early_raw, late_raw)
    factor_four = norm_factor(ffn_raw)
    result = (hidden + ffn_raw * factor_four * scale_four).astype(LOW)

    grad_result = cotangent.astype(WIDE)
    grad_raw, grad_scale_four = norm_back(ffn_raw, factor_four, scale_four, grad_result)
    grad_cols = by_core(grad_raw.astype(LOW))
    half = width // 2
    both_grad = gather_rows(
        jnp.concatenate([grad_cols[:, :half], swap_cores(other_half(grad_cols))]), halves=True
    )
    both_grad = lax.optimization_barrier(both_grad)
    own_down = lax.optimization_barrier(dot_first(both_grad[:length], inner).astype(LOW))
    sum_down = dot_first(both_grad[length:], given) + own_down.astype(WIDE)
    sum_down = sum_down.astype(LOW)
    sum_down, both_grad = after(sum_down, both_grad)
    grad_other = swap_cores(both_grad[length:])
    down_low = plane_sum(sum_down)
    grad_gate, grad_up = inner_back(both_grad, grad_other, w_early, w_late, gate_up)
    send, grad_gate, grad_up = after(product(in_other, grad_gate), grad_gate, grad_up)
    got_gate = swap_cores(send)
    gate_low = None

    def ffn_in_early(*rows):
        nonlocal grad_gate, grad_up, down_low, gate_low
        held = after(grad_gate, *rows)
        sum_gate = product(in_mine, held[0], got_gate)
        held = after(sum_gate, *held[1:])
        sum_gate, grad_gate, grad_up, down_low = after(held[0], grad_gate, grad_up, down_low)
        gate_low = plane_sum(sum_gate)
        return held[1:]

    def ffn_in_rows(start, stop):
        return dot_last(grad_gate[start:stop], w_ffn[:, :hidden_units]) + dot_last(
            grad_up[start:stop], w_ffn[:, hidden_units:]
        )

    grad_ffn_in = scatter_rows(ffn_in_rows, size, ffn_in_early)
    send, grad_up = after(product(in_other, grad_up), grad_up)
    sum_up = product(in_mine, grad_up, swap_cores(send))
    back_three, grad_scale_three = norm_back(hidden, factor_three, scale_three, grad_ffn_in)
    grad_hidden = grad_result + back_three
    back_two, grad_scale_two = norm_back(projected, factor_two, scale_two, grad_hidden)
    up_low = None

    def proj_between(*rows):
        nonlocal up_low
        held = after(sum_up, *rows)
        up_low = plane_sum(held[0])
        return held[1:]

    whole_proj = gather_rows(back_two.astype(LOW), proj_between)
    got, proj_cols = give_core(by_core(whole_proj), mixed)
    sum_output = product_first(proj_cols, mixed, got)
    sum_output, whole_proj = after(sum_output, whole_proj)
    grad_mixed = dot(whole_proj, w_output).astype(LOW)

    grad_linear = attention_back(
        queries, keys, values, grad_mixed, probs, slopes, cosine, sine, q_scale
    )
    got, normed_cols = give_core(normed_cols, grad_linear)
    attn_low = None

    def normed_sent(*rows):
        nonlocal attn_low, gate_low, up_low
        sum_attn = product_first(normed_cols, grad_linear, got)
        sum_attn = jnp.concatenate([sum_attn, sum_output], axis=1)
        sum_attn = after(sum_attn, *rows)[0]
        sum_attn, gate_low, up_low = after(sum_attn, gate_low, up_low)
        attn_low = plane_sum(sum_attn)

    grad_normed = scatter_rows(lambda a, b: dot_last(grad_linear[a:b], w_qkv), size, sent=normed_sent)
    back_one, grad_scale_one = norm_back(inputs, norm_factor(inputs), scale_one, grad_normed)
    grad_tokens = grad_hidden + back_one

    shard_down, shard_gate, shard_up, shard_attn = (
        item.astype(WIDE) for item in (down_low, gate_low, up_low, attn_low)
    )
    shard_query = shard_attn[:, :q_cols]
    shard_output = shard_attn[:, all_cols:]
    shard_key = shard_attn[:, q_cols:first_value]
    shard_value = shard_attn[:, first_value:all_cols]
    if sharing > 1:
        shard_key, shard_value = (
            lax.psum_scatter(
                item.astype(LOW),
                "seq",
                scatter_dimension=1,
                tiled=True,
                axis_index_groups=groups,
            ).astype(WIDE)
            for item in (shard_key, shard_value)
        )

    piece = width // (dp_count * seq_count)
    stacked = jnp.stack([grad_scale_one, grad_scale_two, grad_scale_three, grad_scale_four])
    packed = stacked.reshape(4, dp_count, seq_count, piece).transpose(1, 2, 0, 3)
    packed = packed.reshape(dp_count, seq_count, 4 * piece)
    owned = scatter_small(scatter_small(packed, "dp"), "seq").reshape(4, piece)
    return (
        result,
        grad_tokens,
        shard_query,
        shard_key,
        shard_value,
        shard_output,
        owned[0],
        owned[1],
        owned[2],
        owned[3],
        shard_gate,
        shard_up,
        shard_down,
    )


def solution(mesh):
    rows = P(("dp", "seq"), None)
    weight = P("dp", "seq")
    scale = P("dp")
    scale_grad = P(("dp", "seq"))
    in_specs = (
        (rows,) + (weight,) * 4 + (scale,) * 4 + (weight,) * 3 + (rows,)
    )
    out_specs = (rows, rows) + (weight,) * 4 + (scale_grad,) * 4 + (weight,) * 3
    return jax.shard_map(
        shards, mesh=mesh, in_specs=in_specs, out_specs=out_specs, check_vma=False
    )
```

```python
import functools

import jax
import jax.numpy as jnp
from jax import lax
from jax.experimental import pallas as pl
from jax.experimental.pallas import tpu as pltpu
from jax.sharding import PartitionSpec as P

HQ = 8
HK = 4
HD = 256
WINDOW = 4096
EPSILON = 1e-06
SOFT_CAP = 50.0
LOW = jnp.bfloat16
WIDE = jnp.float32
VMEM_BYTES = 48 * 1024 * 1024


def swap_pairs(count, mask):
    return [(i, i ^ mask) for i in range(count)]


def gather_small(values, axis):
    count = lax.axis_size(axis)
    if count & (count - 1):
        return lax.all_gather(values, axis, axis=0, tiled=False)
    place = lax.axis_index(axis)
    held = values[None]
    bit = 1
    while bit < count:
        other = lax.ppermute(held, axis, swap_pairs(count, bit))
        upper = (place & bit) != 0
        held = jnp.where(
            upper, jnp.concatenate([other, held]), jnp.concatenate([held, other])
        )
        bit *= 2
    return held


def scatter_small(values, axis):
    count = lax.axis_size(axis)
    if count & (count - 1):
        return lax.psum_scatter(values, axis, scatter_dimension=0, tiled=False)
    place = lax.axis_index(axis)
    bit = count // 2
    while bit:
        halves = values.reshape((2, bit) + values.shape[1:])
        upper = (place & bit) != 0
        keep = jnp.where(upper, halves[1], halves[0])
        send = jnp.where(upper, halves[0], halves[1])
        values = keep + lax.ppermute(send, axis, swap_pairs(count, bit))
        bit //= 2
    return values[0]


def square(count):
    return count == 4


def chunk_places(count):
    here = lax.axis_index("seq")
    if square(count):
        return here ^ jnp.arange(count)
    return jnp.arange(count)


def gather_rows(rows, between=None, halves=False):
    count = lax.axis_size("seq")
    if not square(count):
        if between is not None:
            (rows,) = between(rows)
        rows = lax.all_gather(rows, "seq", axis=0, tiled=not halves)
        if halves:
            rows = rows.reshape(count, 2, -1, rows.shape[2]).transpose(1, 0, 2, 3)
            rows = rows.reshape(2, -1, rows.shape[3])
            return rows[0], rows[1]
        return rows
    half = rows.shape[0] // 2
    along, across = swap_pairs(count, 1), swap_pairs(count, 2)
    top, low = rows[:half], rows[half:]
    y_top = lax.ppermute(top, "seq", across)
    x_low = lax.ppermute(low, "seq", along)
    y_low = lax.ppermute(low, "seq", across)
    x_top = lax.ppermute(top, "seq", along)
    if between is not None:
        y_top, x_low = between(y_top, x_low)
    far_top = lax.ppermute(y_top, "seq", along)
    far_low = lax.ppermute(x_low, "seq", across)
    if halves:
        held = after(x_top, y_top, far_top, x_low, y_low)
        first = jnp.concatenate((top,) + held[:3])
        return first, jnp.concatenate((low,) + held[3:] + (far_low,))
    return jnp.concatenate([rows, x_top, x_low, y_top, y_low, far_top, far_low])


def scatter_rows(partial, size, early=None, sent=None):
    count = lax.axis_size("seq")
    if not square(count):
        rows = partial(0, count * size).astype(LOW)
        if early is not None:
            (rows,) = early(rows)
        if sent is not None:
            sent(rows)
        return lax.psum_scatter(rows, "seq", scatter_dimension=0, tiled=True).astype(WIDE)
    half = size // 2
    along, across = swap_pairs(count, 1), swap_pairs(count, 2)
    far = partial(3 * size, 4 * size).astype(LOW)
    via_x = lax.ppermute(far[:half], "seq", along)
    via_y = lax.ppermute(far[half:], "seq", across)
    to_both = partial(size, 3 * size)
    to_x, to_y = to_both[:size], to_both[size:]
    x_top = lax.ppermute(to_x[:half].astype(LOW), "seq", along)
    y_low = lax.ppermute(to_y[half:].astype(LOW), "seq", across)
    if early is not None:
        to_x, to_y = early(to_x, to_y)
    x_low = (to_x[half:] + via_y.astype(WIDE)).astype(LOW)
    y_top = (to_y[:half] + via_x.astype(WIDE)).astype(LOW)
    if sent is not None:
        sent(x_low, y_top)
    x_low = lax.ppermute(x_low, "seq", along)
    y_top = lax.ppermute(y_top, "seq", across)
    own = lax.optimization_barrier(partial(0, size))
    from_x = jnp.concatenate([x_top, x_low]).astype(WIDE)
    from_y = jnp.concatenate([y_top, y_low]).astype(WIDE)
    return own + from_x + from_y


def gather_width(shard):
    return lax.all_gather(shard, "dp", axis=0, tiled=True)


def line_pairs(first, last, step):
    return [(2 * i + c, 2 * (i + step) + c) for i in range(first, last + 1) for c in range(2)]


def core_pairs(planes):
    return swap_pairs(2 * planes, 1)


def row_block(rows):
    return next(size for size in (256, 128, 64, 32, 16) if rows % size == 0)


def column_block(columns):
    return next(size for size in (768, 512, 384, 256, 128) if columns % size == 0)


def this_core():
    return (lax.axis_index("dp") % 2).astype(jnp.int32).reshape(1)


def split_kernel(block, core, rows, parts):
    values = rows[...].astype(WIDE)
    pieces = [values[:, i : i + block] for i in range(0, values.shape[1], block)]
    even = jnp.concatenate(pieces[0::2], axis=1).astype(LOW)
    odd = jnp.concatenate(pieces[1::2], axis=1).astype(LOW)
    half = even.shape[1]

    @pl.when(core[0] == 0)
    def _():
        parts[:, :half] = even
        parts[:, half:] = odd

    @pl.when(core[0] != 0)
    def _():
        parts[:, :half] = odd
        parts[:, half:] = even


def by_core(rows):
    count, width = rows.shape
    size = row_block(count)
    whole = pl.BlockSpec((size, width), lambda i: (i, 0))
    return pl.pallas_call(
        functools.partial(split_kernel, width // lax.axis_size("dp")),
        out_shape=jax.ShapeDtypeStruct((count, width), LOW),
        grid=(count // size,),
        in_specs=[pl.BlockSpec(memory_space=pltpu.SMEM), whole],
        out_specs=whole,
        compiler_params=pltpu.CompilerParams(vmem_limit_bytes=VMEM_BYTES),
        name="split_columns",
    )(this_core(), rows)


def merge_kernel(early, late, out):
    count = lax.axis_size("dp")
    pieces = []
    for i in range(count):
        for part in (early, late):
            block = part.shape[1] // count
            pieces.append(part[:, i * block : (i + 1) * block])
    out[...] = jnp.concatenate(pieces, axis=1)


def merge_columns(early, late):
    count = early.shape[0]
    size = row_block(count)
    columns = early.shape[1] + late.shape[1]
    return pl.pallas_call(
        merge_kernel,
        out_shape=jax.ShapeDtypeStruct((count, columns), WIDE),
        grid=(count // size,),
        in_specs=[pl.BlockSpec((size, part.shape[1]), lambda i: (i, 0)) for part in (early, late)],
        out_specs=pl.BlockSpec((size, columns), lambda i: (i, 0)),
        compiler_params=pltpu.CompilerParams(vmem_limit_bytes=VMEM_BYTES),
        name="merge_columns",
    )(early, late)


def inner_kernel(planes, core, mine, other, w_early, w_late, gate, upward, to_gate, to_up):
    def part(rows, place):
        blocks = []
        for i in range(planes):
            for weight in (w_early, w_late):
                block = weight.shape[0] // planes // 2
                start = pl.multiple_of((2 * i + place) * block, block)
                blocks.append(weight[pl.ds(start, block), :])
        return jnp.dot(rows[...], jnp.concatenate(blocks), preferred_element_type=WIDE)

    grad = part(mine, core[0]) + part(other, 1 - core[0])
    value, slope = gelu_parts(gate[...].astype(WIDE))
    to_gate[...] = (grad * upward[...].astype(WIDE) * slope).astype(LOW)
    to_up[...] = (grad * value).astype(LOW)


def inner_back(mine, other, w_early, w_late, gate_up):
    count, half = other.shape
    units = gate_up.shape[1] // 2
    size = 256 if units % 256 == 0 else 128
    steps = units // size
    rows = pl.BlockSpec((count, half), lambda j: (0, 0))
    part = pl.BlockSpec((count, size), lambda j: (0, j))
    shape = jax.ShapeDtypeStruct((count, units), LOW)
    return pl.pallas_call(
        functools.partial(inner_kernel, lax.axis_size("dp") // 2),
        out_shape=[shape, shape],
        grid=(steps,),
        in_specs=[
            pl.BlockSpec(memory_space=pltpu.SMEM),
            rows,
            rows,
            pl.BlockSpec((w_early.shape[0], size), lambda j: (0, j)),
            pl.BlockSpec((w_late.shape[0], size), lambda j: (0, j)),
            part,
            pl.BlockSpec((count, size), lambda j: (0, j + steps)),
        ],
        out_specs=[part, part],
        compiler_params=pltpu.CompilerParams(vmem_limit_bytes=VMEM_BYTES),
        cost_estimate=pl.CostEstimate(flops=0, bytes_accessed=0, transcendentals=0),
        name="inner_back",
    )(this_core(), mine, other, w_early, w_late, gate_up, gate_up)


def first_kernel(left, right, more, out, turned):
    @pl.when(pl.program_id(0) == 0)
    def _():
        turned[...] = left[...].T

    total = jnp.dot(turned[...], right[...], preferred_element_type=WIDE)
    out[...] = (total + more[...].astype(WIDE)).astype(LOW)


def product_first(left, right, more):
    depth, rows = left.shape[0], left.shape[1] // 2
    columns = right.shape[1]
    size = column_block(columns)
    part = pl.BlockSpec((rows, size), lambda j: (0, j))
    return pl.pallas_call(
        first_kernel,
        out_shape=jax.ShapeDtypeStruct((rows, columns), LOW),
        grid=(columns // size,),
        in_specs=[
            pl.BlockSpec((depth, rows), lambda j: (0, 0)),
            pl.BlockSpec((depth, size), lambda j: (0, j)),
            part,
        ],
        out_specs=part,
        scratch_shapes=[pltpu.VMEM((rows, depth), LOW)],
        compiler_params=pltpu.CompilerParams(vmem_limit_bytes=VMEM_BYTES),
        cost_estimate=pl.CostEstimate(flops=0, bytes_accessed=0, transcendentals=0),
        name="product_first",
    )(left, right, more)


def product_kernel(left, right, *refs):
    total = jnp.dot(left[...], right[...], preferred_element_type=WIDE)
    if len(refs) == 2:
        total = total + refs[0][...].astype(WIDE)
    refs[-1][...] = total.astype(LOW)


def product(left, right, *more):
    rows, depth = left.shape
    columns = right.shape[1]
    size = column_block(columns)
    part = pl.BlockSpec((rows, size), lambda j: (0, j))
    return pl.pallas_call(
        product_kernel,
        out_shape=jax.ShapeDtypeStruct((rows, columns), LOW),
        grid=(columns // size,),
        in_specs=[
            pl.BlockSpec((rows, depth), lambda j: (0, 0)),
            pl.BlockSpec((depth, size), lambda j: (0, j)),
        ]
        + [part] * len(more),
        out_specs=part,
        compiler_params=pltpu.CompilerParams(vmem_limit_bytes=VMEM_BYTES),
        cost_estimate=pl.CostEstimate(flops=0, bytes_accessed=0, transcendentals=0),
        name="product",
    )(left, right, *more)


def attention_back_kernel(
    copies, q_scale, q, k, v, grad, probs, slopes, cosine, sine, out, grad_k, grad_v
):
    head, step = pl.program_id(0), pl.program_id(1)
    size, length = q.shape[0], k.shape[0]
    rows = pl.ds(pl.multiple_of(step * size, size), size)
    low = probs[0]
    grad_probs = dot_last(grad[...], v[...])
    across = jnp.sum(grad_probs * low.astype(WIDE), axis=-1, keepdims=True)
    grad_scores = (slopes[0].astype(WIDE) * (grad_probs - across)).astype(LOW)
    grad_q = rotate(dot(grad_scores, k[...]), cosine[rows, :], -sine[rows, :]) * q_scale
    out[rows, pl.ds(pl.multiple_of(head * HD, HD), HD)] = grad_q.astype(LOW)
    more_k = dot_first(grad_scores, q[...])
    more_v = dot_first(low, grad[...])
    first = (step == 0) & (head % copies == 0)

    @pl.when(first)
    def _():
        grad_k[...] = more_k
        grad_v[...] = more_v

    @pl.when(jnp.logical_not(first))
    def _():
        grad_k[...] += more_k
        grad_v[...] += more_v

    @pl.when((step == length // size - 1) & (head % copies == copies - 1))
    def _():
        heads = pl.num_programs(0)
        place = heads + head // copies
        to_k = pl.ds(pl.multiple_of(place * HD, HD), HD)
        to_v = pl.ds(pl.multiple_of((place + heads // copies) * HD, HD), HD)
        out[:, to_k] = rotate(grad_k[...], cosine[...], -sine[...]).astype(LOW)
        out[:, to_v] = grad_v[...].astype(LOW)


def attention_back(queries, keys, values, grad, probs, slopes, cosine, sine, q_scale):
    length, q_cols = queries.shape
    kv_cols = keys.shape[1]
    heads, copies = q_cols // HD, q_cols // kv_cols
    size = row_block(length)
    by_rows = pl.BlockSpec((size, HD), lambda h, i: (i, h))
    by_kv = pl.BlockSpec((length, HD), lambda h, i: (0, h // copies))
    scores = pl.BlockSpec((1, size, length), lambda h, i: (h, i, 0))
    angle = pl.BlockSpec((length, HD // 2), lambda h, i: (0, 0))
    columns = q_cols + 2 * kv_cols
    return pl.pallas_call(
        functools.partial(attention_back_kernel, copies, q_scale),
        out_shape=jax.ShapeDtypeStruct((length, columns), LOW),
        grid=(heads, length // size),
        in_specs=[by_rows, by_kv, by_kv, by_rows, scores, scores, angle, angle],
        out_specs=pl.BlockSpec((length, columns), lambda h, i: (0, 0)),
        scratch_shapes=[pltpu.VMEM((length, HD), WIDE)] * 2,
        compiler_params=pltpu.CompilerParams(vmem_limit_bytes=VMEM_BYTES),
        cost_estimate=pl.CostEstimate(flops=0, bytes_accessed=0, transcendentals=0),
        name="attention_back",
    )(queries, keys, values, grad, probs, slopes, cosine, sine)


def swap_cores(values):
    return lax.ppermute(values, "dp", core_pairs(lax.axis_size("dp") // 2))


def other_half(columns):
    return columns[:, columns.shape[1] // 2 :]


def give_core(columns, right):
    send = dot_first(other_half(columns), right).astype(LOW)
    send, columns = after(send, columns)
    return swap_cores(send), columns


def plane_sum(both):
    planes = lax.axis_size("dp") // 2
    groups = [[2 * i + c for i in range(planes)] for c in range(2)]
    return lax.psum_scatter(
        both, "dp", scatter_dimension=0, tiled=True, axis_index_groups=groups
    )


def after(value, *before):
    return lax.optimization_barrier((value,) + before)


class LineGather:
    def __init__(self, shard):
        self.planes = lax.axis_size("dp") // 2
        self.shard = self.risen = self.sunk = shard
        self.below, self.above = [], []

    def advance(self, *before):
        step, last = len(self.below), self.planes - 1
        if step == last:
            return
        risen, sunk = after(self.risen, self.sunk, *before)[:2]
        self.risen = lax.ppermute(risen, "dp", line_pairs(step, last - 1, 1))
        self.sunk = lax.ppermute(sunk, "dp", line_pairs(1, last - step, -1))
        self.below.insert(0, self.risen)
        self.above.append(self.sunk)

    def whole(self):
        for _ in range(self.planes - 1):
            self.advance()
        place = lax.axis_index("dp")
        plane, core = place // 2, place % 2
        held = jnp.stack(self.below + [self.shard] + self.above)
        held = lax.dynamic_slice_in_dim(held, self.planes - 1 - plane, self.planes, 0)
        other = swap_cores(held)
        even = jnp.where(core == 0, held, other)
        odd = jnp.where(core == 0, other, held)
        rows = 2 * self.planes * self.shard.shape[0]
        return jnp.stack([even, odd], axis=1).reshape(rows, self.shard.shape[1])


def dot(left, right):
    return jnp.dot(left, right, preferred_element_type=WIDE)


def dot_last(left, right):
    return lax.dot_general(left, right, (((1,), (1,)), ((), ())), preferred_element_type=WIDE)


def dot_first(left, right):
    return lax.dot_general(left, right, (((0,), (0,)), ((), ())), preferred_element_type=WIDE)


def norm_factor(values):
    return lax.rsqrt(jnp.mean(values * values, axis=-1, keepdims=True) + EPSILON)


def norm_back(values, factor, scale, grad):
    scaled = grad * scale
    inner = jnp.mean(scaled * values, axis=-1, keepdims=True)
    back = factor * scaled - values * (factor * factor * factor * inner)
    return back, jnp.sum(grad * values * factor, axis=0)


def rotate(values, cosine, sine):
    half = values.shape[1] // 2
    left = values[:, :half]
    right = values[:, half:]
    return jnp.concatenate([left * cosine - right * sine, right * cosine + left * sine], axis=1)


def gelu_parts(gate):
    scale = 0.7978845608028654
    square_gate = gate * gate
    turn = jnp.tanh(scale * (gate + 0.044715 * (square_gate * gate)))
    value = 0.5 * gate * (1.0 + turn)
    slope = 0.5 * (1.0 + turn) + 0.5 * gate * (1.0 - turn * turn) * (
        scale * (1.0 + 3.0 * 0.044715 * square_gate)
    )
    return value, slope


def shards(
    tokens,
    query_weight,
    key_weight,
    value_weight,
    output_weight,
    attn_norm,
    post_attn_norm,
    ffn_norm,
    post_ffn_norm,
    gate_weight,
    up_weight,
    down_weight,
    cotangent,
):
    size, width = tokens.shape
    seq_count = lax.axis_size("seq")
    dp_count = lax.axis_size("dp")
    heads = HQ // seq_count
    sharing = max(1, seq_count // HK)
    groups = [[first + i for i in range(sharing)] for first in range(0, seq_count, sharing)]
    kv_heads = max(1, HK // seq_count)
    copies = heads // kv_heads

    if sharing > 1:
        key_weight = lax.all_gather(
            key_weight, "seq", axis=1, tiled=True, axis_index_groups=groups
        )
        value_weight = lax.all_gather(
            value_weight, "seq", axis=1, tiled=True, axis_index_groups=groups
        )
    q_cols, kv_cols = heads * HD, kv_heads * HD
    hidden_units = gate_weight.shape[1]
    first_value = q_cols + kv_cols
    all_cols = first_value + kv_cols
    w_attn = gather_width(
        jnp.concatenate([query_weight, key_weight, value_weight, output_weight], axis=1)
    )
    w_ffn = gather_width(jnp.concatenate([gate_weight, up_weight], axis=1))
    early = down_weight.shape[0] * 5 // 9 // 16 * 16
    w_late = gather_width(down_weight[early:])
    w_qkv, w_output = w_attn[:, :all_cols], w_attn[:, all_cols:]

    stacked = jnp.stack([attn_norm, post_attn_norm, ffn_norm, post_ffn_norm])
    scales = gather_small(stacked, "dp").transpose(1, 0, 2).reshape(4, width)
    early_shard, scales = after(down_weight[:early], scales)
    line = LineGather(early_shard)
    line.advance()
    line.advance()
    scales = 1.0 + scales.astype(WIDE)
    scale_one, scale_two, scale_three, scale_four = (scales[i : i + 1] for i in range(4))

    whole_tokens = gather_rows(tokens).astype(WIDE)
    normed = (whole_tokens * norm_factor(whole_tokens) * scale_one).astype(LOW)
    normed_cols = by_core(normed)
    length = size * seq_count
    places = (chunk_places(seq_count)[:, None] * size + jnp.arange(size)[None, :]).reshape(length)
    half = HD // 2
    freqs = 10000.0 ** (-jnp.arange(half).astype(WIDE) / half)
    angles = places.astype(WIDE)[:, None] * freqs[None, :]
    cosine, sine = jnp.cos(angles), jnp.sin(angles)
    allowed = (places[None, :] <= places[:, None]) & (
        places[:, None] - places[None, :] < WINDOW
    )
    q_scale = HD ** (-0.5)
    linear = dot(normed, w_qkv)
    parts = [linear[:, i * HD : (i + 1) * HD] for i in range(heads + 2 * kv_heads)]
    queries = [(rotate(part, cosine, sine) * q_scale).astype(LOW) for part in parts[:heads]]
    keys = [rotate(part, cosine, sine).astype(LOW) for part in parts[heads : heads + kv_heads]]
    values = [part.astype(LOW) for part in parts[heads + kv_heads :]]
    probs, slopes, head_outs = [], [], []
    for h in range(heads):
        turn = jnp.tanh(dot_last(queries[h], keys[h // copies]) / SOFT_CAP)
        capped = jnp.where(allowed, SOFT_CAP * turn, -1e30)
        highest = jnp.max(capped, axis=-1, keepdims=True)
        weights = jnp.exp(capped - highest)
        prob = weights / jnp.sum(weights, axis=-1, keepdims=True)
        probs.append(prob.astype(LOW))
        slopes.append((prob * (1.0 - turn * turn)).astype(LOW))
        head_outs.append(dot(probs[h], values[h // copies]).astype(LOW))
    probs, slopes = jnp.stack(probs), jnp.stack(slopes)
    queries, keys, values = (jnp.concatenate(item, axis=1) for item in (queries, keys, values))
    mixed = jnp.concatenate(head_outs, axis=1)
    mixed, queries, keys, values, probs, slopes = after(
        mixed, queries, keys, values, probs, slopes
    )
    line.advance(mixed)
    w_early = line.whole()
    projected = scatter_rows(lambda a, b: dot_last(mixed[a:b], w_output), size)

    inputs = tokens.astype(WIDE)
    factor_two = norm_factor(projected)
    hidden = inputs + projected * factor_two * scale_two
    factor_three = norm_factor(hidden)
    whole_in = gather_rows((hidden * factor_three * scale_three).astype(LOW))
    gate_up = lax.optimization_barrier(dot(whole_in, w_ffn).astype(LOW))
    gate, upward = gate_up[:, :hidden_units].astype(WIDE), gate_up[:, hidden_units:].astype(WIDE)
    inner = lax.optimization_barrier((gelu_parts(gate)[0] * upward).astype(LOW))
    in_cols = by_core(whole_in)
    in_mine, in_other = in_cols[:, : width // 2].T, other_half(in_cols).T
    in_mine, in_other, inner = after(in_mine, in_other, inner)
    given = swap_cores(inner)

    def early_sent(*rows):
        nonlocal w_late
        w_late = after(w_late, *rows)[0]

    early_raw = scatter_rows(
        lambda a, b: dot_last(inner[a:b], w_early), size, sent=early_sent
    )

    def late_early(*rows):
        nonlocal early_raw
        early_raw, *rows = after(early_raw, *rows)
        return rows

    late_raw = scatter_rows(lambda a, b: dot_last(inner[a:b], w_late), size, late_early)
    ffn_raw = merge_columns(early_raw, late_raw)
    factor_four = norm_factor(ffn_raw)
    result = (hidden + ffn_raw * factor_four * scale_four).astype(LOW)

    grad_result = cotangent.astype(WIDE)
    grad_raw, grad_scale_four = norm_back(ffn_raw, factor_four, scale_four, grad_result)
    grad_cols = by_core(grad_raw.astype(LOW))
    half = width // 2
    own_grad, given_grad = gather_rows(
        jnp.concatenate([grad_cols[:, :half], swap_cores(other_half(grad_cols))]), halves=True
    )
    own_down = lax.optimization_barrier(dot_first(own_grad, inner).astype(LOW))
    sum_down = dot_first(given_grad, given) + own_down.astype(WIDE)
    sum_down = sum_down.astype(LOW)
    sum_down, own_grad, given_grad = after(sum_down, own_grad, given_grad)
    grad_other = swap_cores(given_grad)
    down_low = plane_sum(sum_down)
    grad_gate, grad_up = inner_back(own_grad, grad_other, w_early, w_late, gate_up)
    send, grad_gate, grad_up = after(product(in_other, grad_gate), grad_gate, grad_up)
    got_gate = swap_cores(send)
    gate_low = None

    def ffn_in_early(*rows):
        nonlocal grad_gate, grad_up, down_low, gate_low
        held = after(grad_gate, *rows)
        sum_gate = product(in_mine, held[0], got_gate)
        held = after(sum_gate, *held[1:])
        sum_gate, grad_gate, grad_up, down_low = after(held[0], grad_gate, grad_up, down_low)
        gate_low = plane_sum(sum_gate)
        return held[1:]

    def ffn_in_rows(start, stop):
        return dot_last(grad_gate[start:stop], w_ffn[:, :hidden_units]) + dot_last(
            grad_up[start:stop], w_ffn[:, hidden_units:]
        )

    grad_ffn_in = scatter_rows(ffn_in_rows, size, ffn_in_early)
    send, grad_up = after(product(in_other, grad_up), grad_up)
    sum_up = product(in_mine, grad_up, swap_cores(send))
    back_three, grad_scale_three = norm_back(hidden, factor_three, scale_three, grad_ffn_in)
    grad_hidden = grad_result + back_three
    back_two, grad_scale_two = norm_back(projected, factor_two, scale_two, grad_hidden)
    up_low = None

    def proj_between(*rows):
        nonlocal up_low
        held = after(sum_up, *rows)
        up_low = plane_sum(held[0])
        return held[1:]

    whole_proj = gather_rows(back_two.astype(LOW), proj_between)
    got, proj_cols = give_core(by_core(whole_proj), mixed)
    sum_output = product_first(proj_cols, mixed, got)
    sum_output, whole_proj = after(sum_output, whole_proj)
    grad_mixed = dot(whole_proj, w_output).astype(LOW)

    grad_linear = attention_back(
        queries, keys, values, grad_mixed, probs, slopes, cosine, sine, q_scale
    )
    got, normed_cols = give_core(normed_cols, grad_linear)
    attn_low = None

    def normed_sent(*rows):
        nonlocal attn_low, gate_low, up_low
        sum_attn = product_first(normed_cols, grad_linear, got)
        sum_attn = jnp.concatenate([sum_attn, sum_output], axis=1)
        sum_attn = after(sum_attn, *rows)[0]
        sum_attn, gate_low, up_low = after(sum_attn, gate_low, up_low)
        attn_low = plane_sum(sum_attn)

    grad_normed = scatter_rows(lambda a, b: dot_last(grad_linear[a:b], w_qkv), size, sent=normed_sent)
    back_one, grad_scale_one = norm_back(inputs, norm_factor(inputs), scale_one, grad_normed)
    grad_tokens = grad_hidden + back_one

    shard_down, shard_gate, shard_up, shard_attn = (
        item.astype(WIDE) for item in (down_low, gate_low, up_low, attn_low)
    )
    shard_query = shard_attn[:, :q_cols]
    shard_output = shard_attn[:, all_cols:]
    shard_key = shard_attn[:, q_cols:first_value]
    shard_value = shard_attn[:, first_value:all_cols]
    if sharing > 1:
        shard_key, shard_value = (
            lax.psum_scatter(
                item.astype(LOW),
                "seq",
                scatter_dimension=1,
                tiled=True,
                axis_index_groups=groups,
            ).astype(WIDE)
            for item in (shard_key, shard_value)
        )

    piece = width // (dp_count * seq_count)
    stacked = jnp.stack([grad_scale_one, grad_scale_two, grad_scale_three, grad_scale_four])
    packed = stacked.reshape(4, dp_count, seq_count, piece).transpose(1, 2, 0, 3)
    packed = packed.reshape(dp_count, seq_count, 4 * piece)
    owned = scatter_small(scatter_small(packed, "dp"), "seq").reshape(4, piece)
    return (
        result,
        grad_tokens,
        shard_query,
        shard_key,
        shard_value,
        shard_output,
        owned[0],
        owned[1],
        owned[2],
        owned[3],
        shard_gate,
        shard_up,
        shard_down,
    )


def solution(mesh):
    rows = P(("dp", "seq"), None)
    weight = P("dp", "seq")
    scale = P("dp")
    scale_grad = P(("dp", "seq"))
    in_specs = (
        (rows,) + (weight,) * 4 + (scale,) * 4 + (weight,) * 3 + (rows,)
    )
    out_specs = (rows, rows) + (weight,) * 4 + (scale_grad,) * 4 + (weight,) * 3
    return jax.shard_map(
        shards, mesh=mesh, in_specs=in_specs, out_specs=out_specs, check_vma=False
    )
```
